256 devices in a mesh: dp: 32 (over y, x, core), tensor: 8 (over z).
Axes of the slice: x: 4, y: 4, z: 8, core: 2. Of those that a mesh axis runs over, the one named last changes fastest.
Arguments:
- pool: bfloat16 [1280, 8, 2, 256, 128], P('dp', 'tensor'), may hold values from -6 to 6
- page_map: int32 [1536], P('dp'), may hold values from 0 to 1279, as said below
- branch_len: int32 [1024], P('dp'), may hold values from 1 to 256
- alive: int32 [1024], P('dp'), may hold values 0 or 1
- queries: bfloat16 [1024, 2, 64, 128], P('dp', None, 'tensor'), may hold values from -20 to 20
- new_keys: bfloat16 [1024, 2, 8, 128], P('dp', None, 'tensor'), may hold values from -8 to 8
- new_values: bfloat16 [1024, 2, 8, 128], P('dp', None, 'tensor'), may hold values from -6 to 6
Outputs:
- attended: bfloat16 [1024, 2, 64, 128], P('dp', None, 'tensor')
The draws below stay inside these ranges and needn't reach their ends.
Inputs may be any that keep to these rules, and one draw needn't show every extreme that they name: `page_map`: names one pool page for each slot; every pool page is named by one or two slots; the pages of each dp index (page // 40) are named by 48 slots in all; the prompt slots of one block name at most 1 pages of one dp index and its branch slots at most 1, and in every block one dp index is named by exactly 1 prompt slots and 1 branch slots.
All inputs are finite; a program needn't handle non-finite values. No bound on the sum of `alive` on one device may be relied on, other than what follows from the above.
Results may differ from the reference program's by a relative error of at most 0.009.
Values may be sent and summed in bfloat16 or wider, within the bound.
No kernel may reach another device: no remote copies, remote signals or barrier semaphores. Data moves between devices by JAX's collectives and lax.ppermute only.
A program may use at most 64 MiB of HBM per device.

```python
import jax
import jax.numpy as jnp
from jax import lax

HQ = 64
KVH = 8
HD = 128
PAGE = 256
STEPS = 2
GROUP = 8
PPAGES = 4
BPAGES = 1
ROWS_DEV = 32
ROWS = 1024
RECV = 48
POOL_ROW = 40
N_DP = 32


def plan_pages(key):
    base_key = jax.random.fold_in(key, 101)
    partners = N_DP
    prompt_total = ROWS_DEV // GROUP * PPAGES
    arrangement = jax.random.permutation(jax.random.fold_in(base_key, 1), partners).astype(jnp.int32)
    references = jnp.arange(RECV, dtype=jnp.int32)
    offset_of = jnp.where(references < prompt_total, arrangement[references % partners], arrangement[(references - prompt_total) % partners])
    relabel = jax.random.permutation(jax.random.fold_in(base_key, 2), partners).astype(jnp.int32)
    sources = (relabel[:, None] + offset_of[None, :]) % partners
    doubled = RECV - POOL_ROW
    ref_page = jnp.where(references < 2 * doubled, references // 2, references - doubled)
    shuffle_key = jax.random.fold_in(base_key, 3)

    def shuffle_one(source_id):
        return jax.random.permutation(jax.random.fold_in(shuffle_key, source_id), RECV).astype(jnp.int32)
    shuffled = jax.vmap(shuffle_one)(jnp.arange(partners, dtype=jnp.int32))
    chosen = shuffled[sources, references[None, :]]
    page_ids = ref_page[chosen] + sources * POOL_ROW
    return page_ids.reshape(-1).astype(jnp.int32)


def query_base(key):
    private = jax.random.fold_in(key, 303)
    fluctuation = jax.random.truncated_normal(private, -6.0, 6.0, (STEPS, ROWS, HQ, HD), jnp.float32)
    current = fluctuation[0]
    collected = [current]
    for step_id in range(1, STEPS):
        current = 0.8 * current + 0.6 * fluctuation[step_id]
        collected.append(current)
    return 2.0 * jnp.stack(collected, axis=1)


def draw_page_map(key, part):
    return plan_pages(key)


def draw_pool(key, part):
    private = jax.random.fold_in(key, 3)
    page_ids = jnp.arange(N_DP * POOL_ROW, dtype=jnp.int32)

    def one_page(page):
        page_key = jax.random.fold_in(private, page)
        entries = jax.random.truncated_normal(page_key, -6.0, 6.0, (KVH, 2, PAGE, HD), jnp.float32)
        return entries.astype(jnp.bfloat16)
    return lax.map(one_page, page_ids)


def draw_queries(key, part):
    baseline = query_base(key)
    return baseline.astype(jnp.bfloat16)


def draw_new_keys(key, part):
    baseline = query_base(key)
    grouped = baseline.reshape(ROWS, STEPS, KVH, HQ // KVH, HD)
    folded = 1.2 * jnp.sum(grouped, axis=3) / (2.0 * (HQ // KVH) ** 0.5)
    return jnp.clip(folded, -8.0, 8.0).astype(jnp.bfloat16)


def draw_branch_len(key, part):
    private = jax.random.fold_in(key, 7)
    lengths = jax.random.randint(private, (ROWS,), 1, BPAGES * PAGE + 1)
    positions = jax.random.permutation(jax.random.fold_in(private, 1), ROWS)
    lengths = lengths.at[positions[0]].set(BPAGES * PAGE).at[positions[1]].set(1)
    return lengths.astype(jnp.int32)


def touch_ends(values, key, least, high):
    dims = values.shape
    index_at = [jax.random.randint(jax.random.fold_in(key, axis), (), 0, dims[axis]) for axis in range(len(dims))]
    values = values.at[tuple(index_at)].set(least)
    longest = dims.index(max(dims))
    index_at[longest] = (index_at[longest] + 1) % dims[longest]
    return values.at[tuple(index_at)].set(high)


def block_scale(own_key, extent, shards, low, largest):
    level, own = 1.0, jax.random.fold_in(own_key, 6)
    for dim, shards_of in shards:
        draws = jnp.exp(jax.random.uniform(jax.random.fold_in(own, dim), (shards_of,), jnp.float32, low / len(shards), largest / len(shards)))
        level = level * jnp.repeat(draws, extent[dim] // shards_of).reshape([-1 if axis == dim else 1 for axis in range(len(extent))])
    return level


def centred(stream_key, shape, width, most, shards=(), held_as=jnp.bfloat16):
    loudness = block_scale(stream_key, shape, shards, -0.22, 0.18) if shards else 1.0
    values = jax.random.normal(stream_key, shape, jnp.float32) * width * loudness
    return jnp.minimum(jnp.maximum(values, -most), most).astype(held_as)


def setup_inputs(seed: int = 0) -> dict:
    seeds = jax.random.split(jax.random.key(seed), 8)
    return {
        "pool": draw_pool(jax.random.fold_in(seeds[7], 71), 0),
        "page_map": draw_page_map(jax.random.fold_in(seeds[7], 71), 0),
        "branch_len": draw_branch_len(jax.random.fold_in(seeds[7], 71), 0),
        "alive": touch_ends((jax.random.randint(seeds[3], (ROWS,), 0, 4) < 3).astype(jnp.int32), jax.random.fold_in(seeds[3], 1), 0, 1),
        "queries": draw_queries(jax.random.fold_in(seeds[7], 71), 0),
        "new_keys": draw_new_keys(jax.random.fold_in(seeds[7], 71), 0),
        "new_values": centred(seeds[6], (ROWS, STEPS, KVH, HD), 1.0, 6.0, ((0, 32), (2, 8))),
    }


NEG = -1.0e30


def page_partial(question, page_data, live_count):
    blocks, rows_in, step_count, head_count, head_size = question.shape
    kv_heads = page_data.shape[1]
    grouped = question.reshape(blocks, rows_in, step_count, kv_heads, head_count // kv_heads, head_size).astype(jnp.float32)
    key_rows = page_data[:, :, 0].astype(jnp.float32)
    value_rows = page_data[:, :, 1].astype(jnp.float32)
    scores = jnp.einsum("brskhd,bktd->brskht", grouped, key_rows, precision=lax.Precision.HIGHEST) * (head_size ** -0.5)
    position = lax.broadcasted_iota(jnp.int32, (1, 1, 1, 1, 1, scores.shape[5]), 5)
    usable = position < live_count[:, :, None, None, None, None]
    masked = jnp.where(usable, scores, NEG)
    highest = jnp.max(masked, axis=5)
    weights = jnp.where(usable, jnp.exp(masked - highest[..., None]), 0.0).astype(jnp.bfloat16)
    weights = lax.optimization_barrier(weights).astype(jnp.float32)
    weight_sum = jnp.sum(weights, axis=5)
    blended = jnp.einsum("brskht,bktd->brskhd", weights, value_rows, precision=lax.Precision.HIGHEST)
    return highest, weight_sum, blended


def fresh_partial(question, fresh_keys, fresh_values):
    row_count, step_count, head_count, head_size = question.shape
    kv_heads = fresh_keys.shape[2]
    grouped = question.reshape(row_count, step_count, kv_heads, head_count // kv_heads, head_size).astype(jnp.float32)
    scores = jnp.einsum("rskhd,rukd->rskhu", grouped, fresh_keys.astype(jnp.float32), precision=lax.Precision.HIGHEST) * (head_size ** -0.5)
    later = lax.broadcasted_iota(jnp.int32, (1, step_count, 1, 1, step_count), 4)
    earlier = lax.broadcasted_iota(jnp.int32, (1, step_count, 1, 1, step_count), 1)
    usable = later <= earlier
    masked = jnp.where(usable, scores, NEG)
    highest = jnp.max(masked, axis=4)
    weights = jnp.where(usable, jnp.exp(masked - highest[..., None]), 0.0).astype(jnp.bfloat16)
    weights = lax.optimization_barrier(weights).astype(jnp.float32)
    weight_sum = jnp.sum(weights, axis=4)
    blended = jnp.einsum("rskhu,rukd->rskhd", weights, fresh_values.astype(jnp.float32), precision=lax.Precision.HIGHEST)
    return highest, weight_sum, blended


def arrange(prompt_piece, branch_piece, fresh_piece, groups):
    row_count = fresh_piece.shape[0]
    prompt_rows = prompt_piece.reshape((groups, PPAGES) + prompt_piece.shape[1:])
    prompt_rows = jnp.swapaxes(prompt_rows, 1, 2).reshape((row_count, PPAGES) + prompt_piece.shape[2:])
    branch_rows = branch_piece[:, 0].reshape((row_count, BPAGES) + branch_piece.shape[2:])
    return jnp.concatenate([prompt_rows, branch_rows, fresh_piece[:, None]], axis=1)


def finish(highs, sums, blends, alive):
    ceiling = jnp.max(highs, axis=1, keepdims=True)
    factor = jnp.exp(highs - ceiling)
    weight_sum = jnp.sum(factor * sums, axis=1)
    blended = jnp.sum(factor[..., None] * blends, axis=1)
    result = blended / weight_sum[..., None] * alive.astype(jnp.float32)[:, None, None, None, None]
    row_count, step_count, kv_heads, per_head, head_size = result.shape
    return result.reshape(row_count, step_count, kv_heads * per_head, head_size).astype(jnp.bfloat16)


def attend(page_data, question, lengths, living, fresh_keys, fresh_values):
    row_count = question.shape[0]
    groups = row_count // GROUP
    prompt_slots = groups * PPAGES
    page_size = page_data.shape[3]
    grouped = question.reshape((groups, 1, GROUP) + question.shape[1:])
    prompt_question = jnp.broadcast_to(grouped, (groups, PPAGES, GROUP) + question.shape[1:]).reshape((prompt_slots, GROUP) + question.shape[1:])
    prompt_count = jnp.full((prompt_slots, GROUP), page_size, jnp.int32)
    branch_question = jnp.broadcast_to(question[:, None], (row_count, BPAGES) + question.shape[1:]).reshape((row_count * BPAGES, 1) + question.shape[1:])
    offsets = jnp.arange(BPAGES, dtype=jnp.int32) * page_size
    branch_count = jnp.clip(lengths[:, None] - offsets[None, :], 0, page_size).reshape(-1, 1).astype(jnp.int32)
    prompt_part = page_partial(prompt_question, page_data[:prompt_slots], prompt_count)
    branch_part = page_partial(branch_question, page_data[prompt_slots:], branch_count)
    fresh_part = fresh_partial(question, fresh_keys, fresh_values)
    highs = arrange(prompt_part[0], branch_part[0], fresh_part[0], groups)
    sums = arrange(prompt_part[1], branch_part[1], fresh_part[1], groups)
    blends = arrange(prompt_part[2], branch_part[2], fresh_part[2], groups)
    return finish(highs, sums, blends, living)


def reference(pool, page_map, branch_len, alive, queries, new_keys, new_values):
    def one_block(block_id):
        block_map = lax.dynamic_slice_in_dim(page_map, block_id * RECV, RECV)
        page_data = pool[block_map]
        first_row = block_id * ROWS_DEV
        question = lax.dynamic_slice_in_dim(queries, first_row, ROWS_DEV)
        lengths = lax.dynamic_slice_in_dim(branch_len, first_row, ROWS_DEV)
        living = lax.dynamic_slice_in_dim(alive, first_row, ROWS_DEV)
        fresh_keys = lax.dynamic_slice_in_dim(new_keys, first_row, ROWS_DEV)
        fresh_values = lax.dynamic_slice_in_dim(new_values, first_row, ROWS_DEV)
        return attend(page_data, question, lengths, living, fresh_keys, fresh_values)

    stacked = lax.map(one_block, jnp.arange(N_DP, dtype=jnp.int32))
    return stacked.reshape(ROWS, STEPS, HQ, HD)
```

```python
import jax
import jax.numpy as jnp
from jax import lax
from jax.experimental import pallas as pl
from jax.experimental.pallas import tpu as pltpu
from jax.sharding import PartitionSpec as P

GROUP = 8
PPAGES = 4
POOL_ROW = 40
PAGE = 256
HD = 128
DP = 32
ROWS_DEV = 32
SH = 16
PROMPTS = 16
BRANCH_AT = GROUP * SH
TAIL_AT = BRANCH_AT + SH
MSG = TAIL_AT + SH
NEG = -1e30
LN2 = 0.6931471805599453
SCALE = HD ** (-0.5)
TO_LOG2 = SCALE / LN2
BF = jnp.bfloat16
F32 = jnp.float32
CONTRACT_LAST = (((1,), (1,)), ((), ()))
VMEM = pl.BlockSpec(memory_space=pltpu.VMEM)
SMEM = pl.BlockSpec(memory_space=pltpu.SMEM)
PARAMS = pltpu.CompilerParams(vmem_limit_bytes=40 * 1024 * 1024)


def pack_kernel(map_ref, len_ref, q_ref, out_ref, held_ref):
    lane = lax.broadcasted_iota(jnp.int32, (SH, HD), 1)
    for s in range(DP):
        held_ref[s] = -1
    for j in range(PROMPTS):
        page = map_ref[j]
        s = page // POOL_ROW
        held_ref[s] = page - s * POOL_ROW
        g = j // PPAGES
        for i in range(GROUP):
            out_ref[s, i * SH : (i + 1) * SH, :] = q_ref[g * GROUP + i]
    for e in range(ROWS_DEV):
        page = map_ref[PROMPTS + e]
        s = page // POOL_ROW
        out_ref[s, BRANCH_AT:TAIL_AT, :] = q_ref[e]
        numbers = jnp.where(
            lane == 0, held_ref[s], jnp.where(lane == 1, page - s * POOL_ROW, len_ref[e])
        )
        out_ref[s, TAIL_AT:MSG, :] = numbers.astype(F32).astype(BF)


def attend_kernel(in_ref, pool_ref, out_ref, numbers_v, numbers_s, list_s, stats, sem):
    lane = lax.broadcasted_iota(jnp.int32, (SH, HD), 1)
    token = lax.broadcasted_iota(jnp.int32, (SH, PAGE), 1)
    for b in range(DP):
        numbers_v[b : b + 1, :] = in_ref[b, TAIL_AT:MSG, :].astype(F32)[0:1].astype(jnp.int32)
    copy = pltpu.make_async_copy(numbers_v, numbers_s, sem)
    copy.start()
    stats[...] = jnp.zeros_like(stats)
    copy.wait()
    count = jnp.int32(0)
    for b in range(DP):
        list_s[count] = b
        count = count + jnp.where(numbers_s[b, 0] >= 0, 1, 0)

    def partial(question, page, usable):
        keys = pool_ref[page, 0]
        values = pool_ref[page, 1]
        scores = lax.dot_general(question, keys, CONTRACT_LAST, preferred_element_type=F32)
        if usable is not None:
            scores = jnp.where(usable, scores, NEG)
        highest = jnp.max(scores, axis=1, keepdims=True)
        weights = jnp.exp2((scores - highest) * TO_LOG2).astype(BF)
        total = jnp.sum(weights.astype(F32), axis=1, keepdims=True)
        mix = jnp.dot(weights, values, preferred_element_type=F32)
        return (mix / total).astype(BF), highest * SCALE + jnp.log(total)

    def prompt(j, carry):
        b = list_s[j]
        mix, lse = partial(in_ref[b, 0:BRANCH_AT, :], numbers_s[b, 0], None)
        out_ref[b, 0:BRANCH_AT, :] = mix
        tile = jnp.zeros((SH, HD), F32)
        for i in range(GROUP):
            tile = jnp.where(lane == i, lse[i * SH : (i + 1) * SH], tile)
        stats[b] = tile
        return carry

    lax.fori_loop(0, PROMPTS, prompt, 0, unroll=4)

    def branch(b, carry):
        length = in_ref[b, TAIL_AT:MSG, :].astype(F32)[:, 2:3].astype(jnp.int32)
        mix, lse = partial(in_ref[b, BRANCH_AT:TAIL_AT, :], numbers_s[b, 1], token < length)
        out_ref[b, BRANCH_AT:TAIL_AT, :] = mix
        tile = jnp.where(lane == GROUP, lse, stats[b])
        high = tile.astype(BF).astype(F32)
        rest = tile - high
        middle = rest.astype(BF).astype(F32)
        low = rest - middle
        out_ref[b, TAIL_AT:MSG, :] = (
            high + pltpu.roll(middle, 16, 1) + pltpu.roll(low, 32, 1)
        ).astype(BF)
        return carry

    lax.fori_loop(0, DP, branch, 0, unroll=8)


def combine_kernel(map_ref, alive_ref, in_ref, q_ref, nk_ref, nv_ref, out_ref, fresh_ref):
    lane = lax.broadcasted_iota(jnp.int32, (SH, HD), 1)
    width = nk_ref.shape[0]
    question = q_ref[...].reshape(ROWS_DEV * SH, HD)
    scores = lax.dot_general(question, nk_ref[...], CONTRACT_LAST, preferred_element_type=F32)
    at = lax.broadcasted_iota(jnp.int32, scores.shape, 0)
    new = lax.broadcasted_iota(jnp.int32, scores.shape, 1)
    usable = (at // SH == new // 2) & (new % 2 <= (at % SH) // (SH // 2))
    scores = jnp.where(usable, scores, NEG)
    highest = jnp.max(scores, axis=1, keepdims=True)
    weights = jnp.where(usable, jnp.exp2((scores - highest) * TO_LOG2), 0.0).astype(BF)
    total = jnp.sum(weights.astype(F32), axis=1, keepdims=True)
    mix = jnp.dot(weights, nv_ref[...], preferred_element_type=F32)
    fresh_ref[...] = (mix / total).reshape(ROWS_DEV, SH, HD)
    fresh_lse = highest * SCALE + jnp.log(total)

    def numbers(s):
        tile = in_ref[s, TAIL_AT:MSG, :].astype(F32)
        return tile + pltpu.roll(tile, HD - 16, 1) + pltpu.roll(tile, HD - 32, 1)

    for g in range(ROWS_DEV // GROUP):
        holders = [map_ref[g * PPAGES + k] // POOL_ROW for k in range(PPAGES)]
        levels = [numbers(s) for s in holders]
        own, fresh = jnp.zeros((SH, HD), F32), jnp.zeros((SH, HD), F32)
        homes = []
        for i in range(GROUP):
            row = g * GROUP + i
            s = map_ref[PROMPTS + row] // POOL_ROW
            homes.append(s)
            own = jnp.where(lane == i, numbers(s)[:, GROUP : GROUP + 1], own)
            fresh = jnp.where(lane == i, fresh_lse[row * SH : (row + 1) * SH], fresh)
        levels = levels + [own, fresh]
        peak = levels[0]
        for level in levels[1:]:
            peak = jnp.maximum(peak, level)
        shares = [jnp.exp(level - peak) for level in levels]
        whole = shares[0]
        for share in shares[1:]:
            whole = whole + share
        shares = [share / whole for share in shares]
        for i in range(GROUP):
            row = g * GROUP + i
            parts = [in_ref[s, i * SH : (i + 1) * SH, :].astype(F32) for s in holders]
            parts.append(in_ref[homes[i], BRANCH_AT:TAIL_AT, :].astype(F32))
            parts.append(fresh_ref[row])
            result = shares[0][:, i : i + 1] * parts[0]
            for share, part in zip(shares[1:], parts[1:]):
                result = result + share[:, i : i + 1] * part
            out_ref[row] = (result * alive_ref[row].astype(F32)).astype(BF)


def exchange(message):
    return lax.all_to_all(message, "dp", split_axis=0, concat_axis=0, tiled=True)


def shards(pool, page_map, branch_len, alive, queries, new_keys, new_values):
    message = jax.ShapeDtypeStruct((DP, MSG, HD), BF)
    question = queries.reshape(ROWS_DEV, SH, HD)
    pages = pool.reshape(POOL_ROW, 2, PAGE, HD)
    outgoing = pl.pallas_call(
        pack_kernel,
        out_shape=message,
        in_specs=[SMEM, SMEM, VMEM],
        out_specs=VMEM,
        scratch_shapes=[pltpu.SMEM((DP,), jnp.int32)],
        compiler_params=PARAMS,
        name="pack",
    )(page_map, branch_len, question)
    asked = exchange(outgoing)
    answers = pl.pallas_call(
        attend_kernel,
        out_shape=message,
        in_specs=[VMEM, VMEM],
        out_specs=VMEM,
        scratch_shapes=[
            pltpu.VMEM((DP, HD), jnp.int32),
            pltpu.SMEM((DP, HD), jnp.int32),
            pltpu.SMEM((DP + 8,), jnp.int32),
            pltpu.VMEM((DP, SH, HD), F32),
            pltpu.SemaphoreType.DMA,
        ],
        compiler_params=PARAMS,
        name="attend",
    )(asked, pages)
    incoming = exchange(answers)
    attended = pl.pallas_call(
        combine_kernel,
        out_shape=jax.ShapeDtypeStruct((ROWS_DEV, SH, HD), BF),
        in_specs=[SMEM, SMEM, VMEM, VMEM, VMEM, VMEM],
        out_specs=VMEM,
        scratch_shapes=[pltpu.VMEM((ROWS_DEV, SH, HD), F32)],
        compiler_params=PARAMS,
        name="combine",
    )(
        page_map,
        alive,
        incoming,
        question,
        new_keys.reshape(ROWS_DEV * 2, HD),
        new_values.reshape(ROWS_DEV * 2, HD),
    )
    return attended.reshape(queries.shape)


def solution(mesh):
    return jax.shard_map(
        shards,
        mesh=mesh,
        in_specs=(
            P("dp", "tensor", None, None, None),
            P("dp"),
            P("dp"),
            P("dp"),
            P("dp", None, "tensor", None),
            P("dp", None, "tensor", None),
            P("dp", None, "tensor", None),
        ),
        out_specs=P("dp", None, "tensor", None),
        check_vma=False,
    )
```

```python
import jax
import jax.numpy as jnp
from jax import lax
from jax.experimental import pallas as pl
from jax.experimental.pallas import tpu as pltpu
from jax.sharding import PartitionSpec as P

GROUP = 8
PPAGES = 4
POOL_ROW = 40
PAGE = 256
HD = 128
DP = 32
ROWS_DEV = 32
SH = 16
PROMPTS = 16
BRANCH_AT = GROUP * SH
TAIL_AT = BRANCH_AT + SH
TAIL = 8
MSG = TAIL_AT + TAIL
TOTAL_AT = 10
TERM = 20
NEG = -1e30
LN2 = 0.6931471805599453
SCALE = HD ** (-0.5)
TO_LOG2 = SCALE / LN2
BF = jnp.bfloat16
F32 = jnp.float32
CONTRACT_LAST = (((1,), (1,)), ((), ()))
HBM = pl.BlockSpec(memory_space=pltpu.HBM)
VMEM = pl.BlockSpec(memory_space=pltpu.VMEM)
SMEM = pl.BlockSpec(memory_space=pltpu.SMEM)


def params(mib):
    return pltpu.CompilerParams(vmem_limit_bytes=mib * 1024 * 1024)


def pack_kernel(map_hbm, len_hbm, q_hbm, out_ref, map_ref, len_ref, q_ref, held_ref, sems):
    copies = [
        pltpu.make_async_copy(src, dst, sems.at[n])
        for n, (src, dst) in enumerate(((map_hbm, map_ref), (len_hbm, len_ref), (q_hbm, q_ref)))
    ]
    for copy in copies:
        copy.start()
    row = lax.broadcasted_iota(jnp.int32, (TAIL, HD), 0)
    for s in range(DP):
        held_ref[s] = -1
    for copy in copies:
        copy.wait()
    for j in range(PROMPTS):
        page = map_ref[j]
        s = page // POOL_ROW
        held_ref[s] = page - s * POOL_ROW
        g = j // PPAGES
        for i in range(GROUP):
            out_ref[s, i * SH : (i + 1) * SH, :] = q_ref[g * GROUP + i]
    for e in range(ROWS_DEV):
        page = map_ref[PROMPTS + e]
        s = page // POOL_ROW
        out_ref[s, BRANCH_AT:TAIL_AT, :] = q_ref[e]
        numbers = jnp.where(
            row == 0, held_ref[s], jnp.where(row == 1, page - s * POOL_ROW, len_ref[e])
        )
        out_ref[s, TAIL_AT:MSG, :] = numbers.astype(F32).astype(BF)


def attend_kernel(
    in_ref, pool_ref, out_ref, numbers_v, numbers_s, list_s, scores_ref, weights_ref, maxima, totals, sem
):
    lane = lax.broadcasted_iota(jnp.int32, (SH, HD), 1)
    lane8 = lax.broadcasted_iota(jnp.int32, (TAIL, HD), 1)
    token = lax.broadcasted_iota(jnp.int32, (SH, PAGE), 1)
    ones = jnp.ones((PAGE, HD), BF)
    numbers = jnp.zeros((TAIL, HD), F32)
    for b in range(DP):
        numbers = jnp.where(lane8 == b, in_ref[b, TAIL_AT:MSG, :].astype(F32), numbers)
    numbers_v[...] = numbers.astype(jnp.int32)
    copy = pltpu.make_async_copy(numbers_v, numbers_s, sem)
    copy.start()
    maxima[...] = jnp.zeros_like(maxima)
    totals[...] = jnp.zeros_like(totals)
    copy.wait()
    count = jnp.int32(0)
    for b in range(DP):
        list_s[count] = b
        count = count + jnp.where(numbers_s[0, b] >= 0, 1, 0)

    def raw_scores(question, page):
        return lax.dot_general(question, pool_ref[page, 0], CONTRACT_LAST, preferred_element_type=F32)

    def soft(scores):
        highest = jnp.max(scores, axis=1, keepdims=True)
        return highest, jnp.exp2((scores - highest) * TO_LOG2).astype(BF)

    def blend(weights, page):
        values = jnp.concatenate([pool_ref[page, 1], ones], axis=1)
        both = jnp.dot(weights, values, preferred_element_type=F32)
        return both[:, :HD].astype(BF), both[:, HD:]

    for b in range(DP):
        scores = raw_scores(in_ref[b, BRANCH_AT:TAIL_AT, :], numbers_s[1, b])
        scores_ref[b * SH : (b + 1) * SH, :] = jnp.where(token < numbers_s[2, b], scores, NEG)

    def prompt(j, carry):
        b = list_s[j]
        page = numbers_s[0, b]
        highest, weights = soft(raw_scores(in_ref[b, 0:BRANCH_AT, :], page))
        mix, total = blend(weights, page)
        out_ref[b, 0:BRANCH_AT, :] = mix
        top, whole = jnp.zeros((SH, HD), F32), jnp.zeros((SH, HD), F32)
        for i in range(GROUP):
            top = jnp.where(lane == i, highest[i * SH : (i + 1) * SH], top)
            whole = jnp.where(lane == i, total[i * SH : (i + 1) * SH], whole)
        maxima[b] = top
        totals[b] = whole
        return carry

    lax.fori_loop(0, PROMPTS, prompt, 0, unroll=16)

    highest, weights = soft(scores_ref[...])
    weights_ref[...] = weights
    for b in range(DP):
        mix, total = blend(weights_ref[b * SH : (b + 1) * SH, :], numbers_s[1, b])
        out_ref[b, BRANCH_AT:TAIL_AT, :] = mix
        top = jnp.where(lane == GROUP, highest[b * SH : (b + 1) * SH] * SCALE, maxima[b] * SCALE)
        whole = jnp.where(lane == GROUP, total, totals[b])
        both = top + pltpu.roll(whole, TOTAL_AT, 1)
        both = both[0:TAIL] + pltpu.roll(both[TAIL:SH], HD // 2, 1)
        first = both.astype(BF).astype(F32)
        rest = both - first
        second = rest.astype(BF).astype(F32)
        third = rest - second
        tail = first + pltpu.roll(second, TERM, 1) + pltpu.roll(third, 2 * TERM, 1)
        out_ref[b, TAIL_AT:MSG, :] = tail.astype(BF)


def combine_kernel(
    map_ref, alive_ref, in_ref, q_ref, nk_ref, nv_ref, out_ref, fresh_ref, maxima, totals
):
    lane = lax.broadcasted_iota(jnp.int32, (SH, HD), 1)
    question = q_ref[...].reshape(ROWS_DEV * SH, HD)
    scores = lax.dot_general(question, nk_ref[...], CONTRACT_LAST, preferred_element_type=F32)
    at = lax.broadcasted_iota(jnp.int32, scores.shape, 0)
    new = lax.broadcasted_iota(jnp.int32, scores.shape, 1)
    usable = (at // SH == new // 2) & (new % 2 <= (at % SH) // (SH // 2))
    scores = jnp.where(usable, scores, NEG)
    fresh_top = jnp.max(scores, axis=1, keepdims=True)
    weights = jnp.where(usable, jnp.exp2((scores - fresh_top) * TO_LOG2), 0.0).astype(BF)
    fresh_total = jnp.sum(weights.astype(F32), axis=1, keepdims=True)
    mix = jnp.dot(weights, nv_ref[...], preferred_element_type=F32)
    fresh_ref[...] = mix.reshape(ROWS_DEV, SH, HD)
    fresh_top = fresh_top * SCALE

    for s in range(DP):
        tail = in_ref[s, TAIL_AT:MSG, :].astype(F32)
        tail = tail + pltpu.roll(tail, HD - TERM, 1) + pltpu.roll(tail, HD - 2 * TERM, 1)
        both = jnp.concatenate([tail, pltpu.roll(tail, HD // 2, 1)], axis=0)
        maxima[s] = both
        totals[s] = pltpu.roll(both, HD - TOTAL_AT, 1)

    for g in range(ROWS_DEV // GROUP):
        holders = [map_ref[g * PPAGES + k] // POOL_ROW for k in range(PPAGES)]
        tops = [maxima[s] for s in holders]
        wholes = [totals[s] for s in holders]
        own, own_total, fresh, new_total = (jnp.zeros((SH, HD), F32) for _ in range(4))
        homes = []
        for i in range(GROUP):
            row = g * GROUP + i
            s = map_ref[PROMPTS + row] // POOL_ROW
            homes.append(s)
            own = jnp.where(lane == i, maxima[s][:, GROUP : GROUP + 1], own)
            own_total = jnp.where(lane == i, totals[s][:, GROUP : GROUP + 1], own_total)
            fresh = jnp.where(lane == i, fresh_top[row * SH : (row + 1) * SH], fresh)
            new_total = jnp.where(lane == i, fresh_total[row * SH : (row + 1) * SH], new_total)
        tops = tops + [own, fresh]
        wholes = wholes + [own_total, new_total]
        peak = tops[0]
        for top in tops[1:]:
            peak = jnp.maximum(peak, top)
        shares = [jnp.exp(top - peak) for top in tops]
        whole = shares[0] * wholes[0]
        for share, part in zip(shares[1:], wholes[1:]):
            whole = whole + share * part
        shares = [share / whole for share in shares]
        for i in range(GROUP):
            row = g * GROUP + i
            parts = [in_ref[s, i * SH : (i + 1) * SH, :].astype(F32) for s in holders]
            parts.append(in_ref[homes[i], BRANCH_AT:TAIL_AT, :].astype(F32))
            parts.append(fresh_ref[row])
            result = shares[0][:, i : i + 1] * parts[0]
            for share, part in zip(shares[1:], parts[1:]):
                result = result + share[:, i : i + 1] * part
            out_ref[row] = (result * alive_ref[row].astype(F32)).astype(BF)


def pack(page_map, branch_len, question):
    return pl.pallas_call(
        pack_kernel,
        out_shape=jax.ShapeDtypeStruct((DP, MSG, HD), BF),
        in_specs=[HBM, HBM, HBM],
        out_specs=VMEM,
        scratch_shapes=[
            pltpu.SMEM((ROWS_DEV + PROMPTS,), jnp.int32),
            pltpu.SMEM((ROWS_DEV,), jnp.int32),
            pltpu.VMEM((ROWS_DEV, SH, HD), BF),
            pltpu.SMEM((DP,), jnp.int32),
            pltpu.SemaphoreType.DMA((3,)),
        ],
        compiler_params=params(60),
        name="pack",
    )(page_map, branch_len, question)


def attend(asked, pages):
    return pl.pallas_call(
        attend_kernel,
        out_shape=jax.ShapeDtypeStruct((DP, MSG, HD), BF),
        in_specs=[VMEM, VMEM],
        out_specs=VMEM,
        scratch_shapes=[
            pltpu.VMEM((TAIL, HD), jnp.int32),
            pltpu.SMEM((TAIL, HD), jnp.int32),
            pltpu.SMEM((DP + 8,), jnp.int32),
            pltpu.VMEM((DP * SH, PAGE), F32),
            pltpu.VMEM((DP * SH, PAGE), BF),
            pltpu.VMEM((DP, SH, HD), F32),
            pltpu.VMEM((DP, SH, HD), F32),
            pltpu.SemaphoreType.DMA,
        ],
        compiler_params=params(20),
        name="attend",
    )(asked, pages)


def combine(page_map, alive, incoming, question, new_keys, new_values):
    return pl.pallas_call(
        combine_kernel,
        out_shape=jax.ShapeDtypeStruct((ROWS_DEV, SH, HD), BF),
        in_specs=[SMEM, SMEM, VMEM, VMEM, VMEM, VMEM],
        out_specs=VMEM,
        scratch_shapes=[pltpu.VMEM((ROWS_DEV, SH, HD), F32)] + [pltpu.VMEM((DP, SH, HD), F32)] * 2,
        compiler_params=params(20),
        name="combine",
    )(page_map, alive, incoming, question, new_keys, new_values)


def exchange(message):
    return lax.all_to_all(message, "dp", split_axis=0, concat_axis=0, tiled=True)


def shards(pool, page_map, branch_len, alive, queries, new_keys, new_values):
    question = queries.reshape(ROWS_DEV, SH, HD)
    asked = exchange(pack(page_map, branch_len, question))
    incoming = exchange(attend(asked, pool.reshape(POOL_ROW, 2, PAGE, HD)))
    new_keys = new_keys.reshape(ROWS_DEV * 2, HD)
    new_values = new_values.reshape(ROWS_DEV * 2, HD)
    attended = combine(page_map, alive, incoming, question, new_keys, new_values)
    return attended.reshape(queries.shape)


def solution(mesh):
    return jax.shard_map(
        shards,
        mesh=mesh,
        in_specs=(
            P("dp", "tensor", None, None, None),
            P("dp"),
            P("dp"),
            P("dp"),
            P("dp", None, "tensor", None),
            P("dp", None, "tensor", None),
            P("dp", None, "tensor", None),
        ),
        out_specs=P("dp", None, "tensor", None),
        check_vma=False,
    )
```

```python
import jax
import jax.numpy as jnp
from jax import lax
from jax.experimental import pallas as pl
from jax.experimental.pallas import tpu as pltpu
from jax.sharding import PartitionSpec as P

GROUP = 8
PPAGES = 4
POOL_ROW = 40
PAGE = 256
HD = 128
DP = 32
ROWS_DEV = 32
SH = 16
PROMPTS = 16
BRANCH_AT = GROUP * SH
TAIL_AT = BRANCH_AT + SH
TAIL = 8
LENGTHS_AT = PROMPTS + ROWS_DEV
ALIVE_AT = LENGTHS_AT + ROWS_DEV
MSG = TAIL_AT + TAIL
TOTAL_AT = 10
TERM = 20
NEG = -1e30
LN2 = 0.6931471805599453
SCALE = HD ** (-0.5)
TO_LOG2 = SCALE / LN2
BF = jnp.bfloat16
F32 = jnp.float32
CONTRACT_LAST = (((1,), (1,)), ((), ()))
VMEM = pl.BlockSpec(memory_space=pltpu.VMEM)
SMEM = pl.BlockSpec(memory_space=pltpu.SMEM)


def params(mib):
    return pltpu.CompilerParams(vmem_limit_bytes=mib * 1024 * 1024)


def pack_kernel(num_ref, q_ref, out_ref, held_ref):
    row = lax.broadcasted_iota(jnp.int32, (TAIL, HD), 0)
    for s in range(DP):
        held_ref[s] = -1
    for j in range(PROMPTS):
        page = num_ref[j]
        s = page // POOL_ROW
        held_ref[s] = page - s * POOL_ROW
        g = j // PPAGES
        for i in range(GROUP):
            out_ref[s, i * SH : (i + 1) * SH, :] = q_ref[g * GROUP + i]
    for e in range(ROWS_DEV):
        page = num_ref[PROMPTS + e]
        s = page // POOL_ROW
        out_ref[s, BRANCH_AT:TAIL_AT, :] = q_ref[e]
        numbers = jnp.where(
            row == 0, held_ref[s], jnp.where(row == 1, page - s * POOL_ROW, num_ref[LENGTHS_AT + e])
        )
        out_ref[s, TAIL_AT:MSG, :] = numbers.astype(F32).astype(BF)


def attend_kernel(
    in_ref, pool_ref, out_ref, numbers_v, numbers_s, list_s, scores_ref, weights_ref, maxima, totals, sem
):
    lane = lax.broadcasted_iota(jnp.int32, (SH, HD), 1)
    lane8 = lax.broadcasted_iota(jnp.int32, (TAIL, HD), 1)
    token = lax.broadcasted_iota(jnp.int32, (SH, PAGE), 1)
    ones = jnp.ones((PAGE, HD), BF)
    numbers = jnp.zeros((TAIL, HD), F32)
    for b in range(DP):
        numbers = jnp.where(lane8 == b, in_ref[b, TAIL_AT:MSG, :].astype(F32), numbers)
    numbers_v[...] = numbers.astype(jnp.int32)
    copy = pltpu.make_async_copy(numbers_v, numbers_s, sem)
    copy.start()
    maxima[...] = jnp.zeros_like(maxima)
    totals[...] = jnp.zeros_like(totals)
    copy.wait()
    count = jnp.int32(0)
    for b in range(DP):
        list_s[count] = b
        count = count + jnp.where(numbers_s[0, b] >= 0, 1, 0)

    def raw_scores(question, page):
        return lax.dot_general(question, pool_ref[page, 0], CONTRACT_LAST, preferred_element_type=F32)

    def soft(scores):
        highest = jnp.max(scores, axis=1, keepdims=True)
        return highest, jnp.exp2((scores - highest) * TO_LOG2).astype(BF)

    def blend(weights, page):
        values = jnp.concatenate([pool_ref[page, 1], ones], axis=1)
        both = jnp.dot(weights, values, preferred_element_type=F32)
        return both[:, :HD].astype(BF), both[:, HD:]

    for b in range(DP):
        scores = raw_scores(in_ref[b, BRANCH_AT:TAIL_AT, :], numbers_s[1, b])
        scores_ref[b * SH : (b + 1) * SH, :] = jnp.where(token < numbers_s[2, b], scores, NEG)

    def prompt(j, carry):
        b = list_s[j]
        page = numbers_s[0, b]
        highest, weights = soft(raw_scores(in_ref[b, 0:BRANCH_AT, :], page))
        mix, total = blend(weights, page)
        out_ref[b, 0:BRANCH_AT, :] = mix
        top, whole = jnp.zeros((SH, HD), F32), jnp.zeros((SH, HD), F32)
        for i in range(GROUP):
            top = jnp.where(lane == i, highest[i * SH : (i + 1) * SH], top)
            whole = jnp.where(lane == i, total[i * SH : (i + 1) * SH], whole)
        maxima[b] = top
        totals[b] = whole
        return carry

    lax.fori_loop(0, PROMPTS, prompt, 0, unroll=16)

    highest, weights = soft(scores_ref[...])
    weights_ref[...] = weights
    for b in range(DP):
        mix, total = blend(weights_ref[b * SH : (b + 1) * SH, :], numbers_s[1, b])
        out_ref[b, BRANCH_AT:TAIL_AT, :] = mix
        top = jnp.where(lane == GROUP, highest[b * SH : (b + 1) * SH] * SCALE, maxima[b] * SCALE)
        whole = jnp.where(lane == GROUP, total, totals[b])
        both = top + pltpu.roll(whole, TOTAL_AT, 1)
        both = both[0:TAIL] + pltpu.roll(both[TAIL:SH], HD // 2, 1)
        first = both.astype(BF).astype(F32)
        rest = both - first
        second = rest.astype(BF).astype(F32)
        third = rest - second
        tail = first + pltpu.roll(second, TERM, 1) + pltpu.roll(third, 2 * TERM, 1)
        out_ref[b, TAIL_AT:MSG, :] = tail.astype(BF)


def combine_kernel(
    num_ref, in_ref, q_ref, nk_ref, nv_ref, out_ref, fresh_ref, maxima, totals
):
    lane = lax.broadcasted_iota(jnp.int32, (SH, HD), 1)
    question = q_ref[...].reshape(ROWS_DEV * SH, HD)
    scores = lax.dot_general(question, nk_ref[...], CONTRACT_LAST, preferred_element_type=F32)
    at = lax.broadcasted_iota(jnp.int32, scores.shape, 0)
    new = lax.broadcasted_iota(jnp.int32, scores.shape, 1)
    usable = (at // SH == new // 2) & (new % 2 <= (at % SH) // (SH // 2))
    scores = jnp.where(usable, scores, NEG)
    fresh_top = jnp.max(scores, axis=1, keepdims=True)
    weights = jnp.where(usable, jnp.exp2((scores - fresh_top) * TO_LOG2), 0.0).astype(BF)
    fresh_total = jnp.sum(weights.astype(F32), axis=1, keepdims=True)
    mix = jnp.dot(weights, nv_ref[...], preferred_element_type=F32)
    fresh_ref[...] = mix.reshape(ROWS_DEV, SH, HD)
    fresh_top = fresh_top * SCALE

    for s in range(DP):
        tail = in_ref[s, TAIL_AT:MSG, :].astype(F32)
        tail = tail + pltpu.roll(tail, HD - TERM, 1) + pltpu.roll(tail, HD - 2 * TERM, 1)
        both = jnp.concatenate([tail, pltpu.roll(tail, HD // 2, 1)], axis=0)
        maxima[s] = both
        totals[s] = pltpu.roll(both, HD - TOTAL_AT, 1)

    for g in range(ROWS_DEV // GROUP):
        holders = [num_ref[g * PPAGES + k] // POOL_ROW for k in range(PPAGES)]
        tops = [maxima[s] for s in holders]
        wholes = [totals[s] for s in holders]
        own, own_total, fresh, new_total = (jnp.zeros((SH, HD), F32) for _ in range(4))
        homes = []
        for i in range(GROUP):
            row = g * GROUP + i
            s = num_ref[PROMPTS + row] // POOL_ROW
            homes.append(s)
            own = jnp.where(lane == i, maxima[s][:, GROUP : GROUP + 1], own)
            own_total = jnp.where(lane == i, totals[s][:, GROUP : GROUP + 1], own_total)
            fresh = jnp.where(lane == i, fresh_top[row * SH : (row + 1) * SH], fresh)
            new_total = jnp.where(lane == i, fresh_total[row * SH : (row + 1) * SH], new_total)
        tops = tops + [own, fresh]
        wholes = wholes + [own_total, new_total]
        peak = tops[0]
        for top in tops[1:]:
            peak = jnp.maximum(peak, top)
        shares = [jnp.exp(top - peak) for top in tops]
        whole = shares[0] * wholes[0]
        for share, part in zip(shares[1:], wholes[1:]):
            whole = whole + share * part
        shares = [share / whole for share in shares]
        for i in range(GROUP):
            row = g * GROUP + i
            parts = [in_ref[s, i * SH : (i + 1) * SH, :].astype(F32) for s in holders]
            parts.append(in_ref[homes[i], BRANCH_AT:TAIL_AT, :].astype(F32))
            parts.append(fresh_ref[row])
            result = shares[0][:, i : i + 1] * parts[0]
            for share, part in zip(shares[1:], parts[1:]):
                result = result + share[:, i : i + 1] * part
            out_ref[row] = (result * num_ref[ALIVE_AT + row].astype(F32)).astype(BF)


def pack(integers, question):
    return pl.pallas_call(
        pack_kernel,
        out_shape=jax.ShapeDtypeStruct((DP, MSG, HD), BF),
        in_specs=[SMEM, VMEM],
        out_specs=VMEM,
        scratch_shapes=[pltpu.SMEM((DP,), jnp.int32)],
        compiler_params=params(8),
        cost_estimate=pl.CostEstimate(flops=10**11, bytes_accessed=10**8, transcendentals=0),
        name="pack",
    )(integers, question)


def attend(asked, pages):
    return pl.pallas_call(
        attend_kernel,
        out_shape=jax.ShapeDtypeStruct((DP, MSG, HD), BF),
        in_specs=[VMEM, VMEM],
        out_specs=VMEM,
        scratch_shapes=[
            pltpu.VMEM((TAIL, HD), jnp.int32),
            pltpu.SMEM((TAIL, HD), jnp.int32),
            pltpu.SMEM((DP + 8,), jnp.int32),
            pltpu.VMEM((DP * SH, PAGE), F32),
            pltpu.VMEM((DP * SH, PAGE), BF),
            pltpu.VMEM((DP, SH, HD), F32),
            pltpu.VMEM((DP, SH, HD), F32),
            pltpu.SemaphoreType.DMA,
        ],
        compiler_params=params(20),
        name="attend",
    )(asked, pages)


def combine(integers, incoming, question, new_keys, new_values):
    return pl.pallas_call(
        combine_kernel,
        out_shape=jax.ShapeDtypeStruct((ROWS_DEV, SH, HD), BF),
        in_specs=[SMEM, VMEM, VMEM, VMEM, VMEM],
        out_specs=VMEM,
        scratch_shapes=[pltpu.VMEM((ROWS_DEV, SH, HD), F32)] + [pltpu.VMEM((DP, SH, HD), F32)] * 2,
        compiler_params=params(20),
        name="combine",
    )(integers, incoming, question, new_keys, new_values)


def exchange(message):
    return lax.all_to_all(message, "dp", split_axis=0, concat_axis=0, tiled=True)


def shards(pool, page_map, branch_len, alive, queries, new_keys, new_values):
    question = queries.reshape(ROWS_DEV, SH, HD)
    integers = jnp.concatenate([page_map, branch_len, alive])
    asked = exchange(pack(integers, question))
    incoming = exchange(attend(asked, pool.reshape(POOL_ROW, 2, PAGE, HD)))
    new_keys = new_keys.reshape(ROWS_DEV * 2, HD)
    new_values = new_values.reshape(ROWS_DEV * 2, HD)
    attended = combine(integers, incoming, question, new_keys, new_values)
    return attended.reshape(queries.shape)


def solution(mesh):
    return jax.shard_map(
        shards,
        mesh=mesh,
        in_specs=(
            P("dp", "tensor", None, None, None),
            P("dp"),
            P("dp"),
            P("dp"),
            P("dp", None, "tensor", None),
            P("dp", None, "tensor", None),
            P("dp", None, "tensor", None),
        ),
        out_specs=P("dp", None, "tensor", None),
        check_vma=False,
    )
```

```python
import jax
import jax.numpy as jnp
from jax import lax
from jax.experimental import pallas as pl
from jax.experimental.pallas import tpu as pltpu
from jax.sharding import PartitionSpec as P

GROUP = 8
PPAGES = 4
POOL_ROW = 40
PAGE = 256
HD = 128
DP = 32
ROWS_DEV = 32
SH = 16
PROMPTS = 16
BRANCH_AT = GROUP * SH
TAIL_AT = BRANCH_AT + SH
TAIL = 8
MSG = TAIL_AT + TAIL
TOTAL_AT = 32
TERM = 10
NEG = -1e30
LN2 = 0.6931471805599453
SCALE = HD ** (-0.5)
TO_LOG2 = SCALE / LN2
BF = jnp.bfloat16
F32 = jnp.float32
CONTRACT_LAST = (((1,), (1,)), ((), ()))
VMEM = pl.BlockSpec(memory_space=pltpu.VMEM)
SMEM = pl.BlockSpec(memory_space=pltpu.SMEM)


def params(mib):
    return pltpu.CompilerParams(vmem_limit_bytes=mib * 1024 * 1024)


def blank_kernel(held_ref):
    held_ref[...] = jnp.full(held_ref.shape, -1, jnp.int32)


def pack_kernel(map_ref, len_ref, blank_ref, q_ref, out_ref, held_ref):
    row = lax.broadcasted_iota(jnp.int32, (TAIL, HD), 0)
    for s in range(DP):
        held_ref[s] = blank_ref[0, s]
    for j in range(PROMPTS):
        page = map_ref[j]
        s = page // POOL_ROW
        held_ref[s] = page - s * POOL_ROW
        g = j // PPAGES
        for i in range(GROUP):
            out_ref[s, i * SH : (i + 1) * SH, :] = q_ref[g * GROUP + i]
    for e in range(ROWS_DEV):
        page = map_ref[PROMPTS + e]
        s = page // POOL_ROW
        out_ref[s, BRANCH_AT:TAIL_AT, :] = q_ref[e]
        numbers = jnp.where(
            row == 0, held_ref[s], jnp.where(row == 1, page - s * POOL_ROW, len_ref[e])
        )
        out_ref[s, TAIL_AT:MSG, :] = numbers.astype(F32).astype(BF)


def attend_kernel(
    in_ref, pool_ref, out_ref, numbers_s, list_s, scores_ref, weights_ref, maxima, totals
):
    lane = lax.broadcasted_iota(jnp.int32, (SH, HD), 1)
    token = lax.broadcasted_iota(jnp.int32, (SH, PAGE), 1)
    ones = jnp.ones((PAGE, HD), BF)
    count = jnp.int32(0)
    for b in range(DP):
        numbers = in_ref[b, TAIL_AT:MSG, :].astype(F32).astype(jnp.int32)
        list_s[count] = b
        count = count + jnp.where(numbers[0, 0] >= 0, 1, 0)
        for k in range(3):
            numbers_s[k, b] = numbers[k, 0]
    maxima[...] = jnp.zeros_like(maxima)
    totals[...] = jnp.zeros_like(totals)

    def raw_scores(question, page):
        return lax.dot_general(question, pool_ref[page, 0], CONTRACT_LAST, preferred_element_type=F32)

    def soft(scores):
        highest = jnp.max(scores, axis=1, keepdims=True)
        return highest, jnp.exp2((scores - highest) * TO_LOG2).astype(BF)

    def blend(weights, page):
        values = jnp.concatenate([pool_ref[page, 1], ones], axis=1)
        both = jnp.dot(weights, values, preferred_element_type=F32)
        return both[:, :HD].astype(BF), both[:, HD:]

    for b in range(DP):
        scores = raw_scores(in_ref[b, BRANCH_AT:TAIL_AT, :], numbers_s[1, b])
        scores_ref[b * SH : (b + 1) * SH, :] = jnp.where(token < numbers_s[2, b], scores, NEG)

    def prompt(j, carry):
        b = list_s[j]
        page = numbers_s[0, b]
        highest, weights = soft(raw_scores(in_ref[b, 0:BRANCH_AT, :], page))
        mix, total = blend(weights, page)
        out_ref[b, 0:BRANCH_AT, :] = mix
        top, whole = jnp.zeros((SH, HD), F32), jnp.zeros((SH, HD), F32)
        for i in range(GROUP):
            top = jnp.where(lane == i, highest[i * SH : (i + 1) * SH], top)
            whole = jnp.where(lane == i, total[i * SH : (i + 1) * SH], whole)
        maxima[b] = top
        totals[b] = whole
        return carry

    lax.fori_loop(0, PROMPTS, prompt, 0, unroll=16)

    highest, weights = soft(scores_ref[...])
    weights_ref[...] = weights
    total = jnp.sum(weights.astype(F32), axis=1, keepdims=True)
    for b in range(DP):
        values = pool_ref[numbers_s[1, b], 1]
        mix = jnp.dot(weights_ref[b * SH : (b + 1) * SH, :], values, preferred_element_type=F32)
        out_ref[b, BRANCH_AT:TAIL_AT, :] = mix.astype(BF)
        top = jnp.where(lane == GROUP, highest[b * SH : (b + 1) * SH] * SCALE, maxima[b] * SCALE)
        whole = jnp.where(lane == GROUP, total[b * SH : (b + 1) * SH], totals[b])
        both = top + pltpu.roll(whole, TOTAL_AT, 1)
        both = both[0:TAIL] + pltpu.roll(both[TAIL:SH], HD // 2, 1)
        first = both.astype(BF).astype(F32)
        rest = both - first
        second = rest.astype(BF).astype(F32)
        third = rest - second
        tail = first + pltpu.roll(second, TERM, 1) + pltpu.roll(third, 2 * TERM, 1)
        out_ref[b, TAIL_AT:MSG, :] = tail.astype(BF)


def combine_kernel(
    map_ref, alive_ref, in_ref, q_ref, nk_ref, nv_ref, out_ref, fresh_ref, numbers_ref
):
    half = SH // 2
    lane = lax.broadcasted_iota(jnp.int32, (half, HD), 1)
    place = lane % TOTAL_AT
    question = q_ref[...].reshape(ROWS_DEV * SH, HD)
    scores = lax.dot_general(question, nk_ref[...], CONTRACT_LAST, preferred_element_type=F32)
    at = lax.broadcasted_iota(jnp.int32, scores.shape, 0)
    new = lax.broadcasted_iota(jnp.int32, scores.shape, 1)
    usable = (at // SH == new // 2) & (new % 2 <= (at % SH) // half)
    scores = jnp.where(usable, scores, NEG)
    top = jnp.max(scores, axis=1, keepdims=True)
    weights = jnp.where(usable, jnp.exp2((scores - top) * TO_LOG2), 0.0).astype(BF)
    total = jnp.sum(weights.astype(F32), axis=1, keepdims=True)
    mix = jnp.dot(weights, nv_ref[...], preferred_element_type=F32)
    fresh_ref[...] = mix.reshape(ROWS_DEV, SH, HD)
    top = top * SCALE

    fresh = jnp.zeros((half, HD), F32)
    for r in range(ROWS_DEV):
        for n, column in enumerate((top, total)):
            for m in range(2):
                piece = column[r * SH + m * half : r * SH + (m + 1) * half]
                fresh = jnp.where(lane == m * HD // 2 + n * TOTAL_AT + r, piece, fresh)

    for s in range(DP):
        tail = in_ref[s, TAIL_AT:MSG, :].astype(F32)
        numbers_ref[s] = tail + pltpu.roll(tail, HD - TERM, 1) + pltpu.roll(tail, HD - 2 * TERM, 1)

    holders = [map_ref[j] // POOL_ROW for j in range(PROMPTS + ROWS_DEV)]
    blocks = []
    for k in range(PPAGES):
        block = numbers_ref[holders[k]]
        for g in range(1, ROWS_DEV // GROUP):
            own = pltpu.roll(numbers_ref[holders[g * PPAGES + k]], g * GROUP, 1)
            block = jnp.where(place // GROUP == g, own, block)
        blocks.append(block)
    block = jnp.zeros((half, HD), F32)
    for r in range(ROWS_DEV):
        own = pltpu.roll(numbers_ref[holders[PROMPTS + r]], (r - GROUP) % HD, 1)
        block = jnp.where(place == r, own, block)
    blocks += [block, fresh]

    peak = blocks[0]
    for block in blocks[1:]:
        peak = jnp.maximum(peak, block)
    shares = [jnp.exp(block - peak) for block in blocks]
    wholes = [share * pltpu.roll(block, HD - TOTAL_AT, 1) for share, block in zip(shares, blocks)]
    whole = wholes[0]
    for part in wholes[1:]:
        whole = whole + part
    shares = [share / whole for share in shares]

    for r in range(ROWS_DEV):
        g, i = r // GROUP, r % GROUP
        parts = [
            in_ref[holders[g * PPAGES + k], i * SH : (i + 1) * SH, :].astype(F32)
            for k in range(PPAGES)
        ]
        parts.append(in_ref[holders[PROMPTS + r], BRANCH_AT:TAIL_AT, :].astype(F32))
        parts.append(fresh_ref[r])
        result = None
        for share, part in zip(shares, parts):
            column = jnp.concatenate(
                [share[:, r : r + 1], share[:, HD // 2 + r : HD // 2 + r + 1]], axis=0
            )
            result = column * part if result is None else result + column * part
        out_ref[r] = (result * alive_ref[r].astype(F32)).astype(BF)


def blank():
    return pl.pallas_call(
        blank_kernel,
        out_shape=jax.ShapeDtypeStruct((1, HD), jnp.int32),
        out_specs=VMEM,
        compiler_params=params(8),
        cost_estimate=pl.CostEstimate(flops=10**11, bytes_accessed=10**8, transcendentals=0),
        name="blank",
    )()


def pack(page_map, branch_len, question):
    return pl.pallas_call(
        pack_kernel,
        out_shape=jax.ShapeDtypeStruct((DP, MSG, HD), BF),
        in_specs=[SMEM, SMEM, SMEM, VMEM],
        out_specs=VMEM,
        scratch_shapes=[pltpu.SMEM((DP,), jnp.int32)],
        compiler_params=params(8),
        cost_estimate=pl.CostEstimate(flops=10**11, bytes_accessed=10**8, transcendentals=0),
        name="pack",
    )(page_map, branch_len, blank(), question)


def attend(asked, pages):
    return pl.pallas_call(
        attend_kernel,
        out_shape=jax.ShapeDtypeStruct((DP, MSG, HD), BF),
        in_specs=[VMEM, VMEM],
        out_specs=VMEM,
        scratch_shapes=[
            pltpu.SMEM((3, DP), jnp.int32),
            pltpu.SMEM((DP + 8,), jnp.int32),
            pltpu.VMEM((DP * SH, PAGE), F32),
            pltpu.VMEM((DP * SH, PAGE), BF),
            pltpu.VMEM((DP, SH, HD), F32),
            pltpu.VMEM((DP, SH, HD), F32),
        ],
        compiler_params=params(20),
        name="attend",
    )(asked, pages)


def combine(page_map, alive, incoming, question, new_keys, new_values):
    return pl.pallas_call(
        combine_kernel,
        out_shape=jax.ShapeDtypeStruct((ROWS_DEV, SH, HD), BF),
        in_specs=[SMEM, SMEM, VMEM, VMEM, VMEM, VMEM],
        out_specs=VMEM,
        scratch_shapes=[pltpu.VMEM((ROWS_DEV, SH, HD), F32), pltpu.VMEM((DP, TAIL, HD), F32)],
        compiler_params=params(20),
        name="combine",
    )(page_map, alive, incoming, question, new_keys, new_values)


def exchange(message):
    return lax.all_to_all(message, "dp", split_axis=0, concat_axis=0, tiled=True)


def shards(pool, page_map, branch_len, alive, queries, new_keys, new_values):
    question = queries.reshape(ROWS_DEV, SH, HD)
    asked = exchange(pack(page_map, branch_len, question))
    incoming = exchange(attend(asked, pool.reshape(POOL_ROW, 2, PAGE, HD)))
    new_keys = new_keys.reshape(ROWS_DEV * 2, HD)
    new_values = new_values.reshape(ROWS_DEV * 2, HD)
    attended = combine(page_map, alive, incoming, question, new_keys, new_values)
    return attended.reshape(queries.shape)


def solution(mesh):
    return jax.shard_map(
        shards,
        mesh=mesh,
        in_specs=(
            P("dp", "tensor", None, None, None),
            P("dp"),
            P("dp"),
            P("dp"),
            P("dp", None, "tensor", None),
            P("dp", None, "tensor", None),
            P("dp", None, "tensor", None),
        ),
        out_specs=P("dp", None, "tensor", None),
        check_vma=False,
    )
```

```python
import jax
import jax.numpy as jnp
from jax import lax
from jax.experimental import pallas as pl
from jax.experimental.pallas import tpu as pltpu
from jax.sharding import PartitionSpec as P

GROUP = 8
PPAGES = 4
POOL_ROW = 40
PAGE = 256
HD = 128
DP = 32
ROWS_DEV = 32
SH = 16
PROMPTS = 16
BRANCH_AT = GROUP * SH
TAIL_AT = BRANCH_AT + SH
TAIL = 8
MSG = TAIL_AT + TAIL
TOTAL_AT = 32
TERM = 10
NEG = -1e30
LN2 = 0.6931471805599453
SCALE = HD ** (-0.5)
TO_LOG2 = SCALE / LN2
BF = jnp.bfloat16
F32 = jnp.float32
CONTRACT_LAST = (((1,), (1,)), ((), ()))
VMEM = pl.BlockSpec(memory_space=pltpu.VMEM)
SMEM = pl.BlockSpec(memory_space=pltpu.SMEM)


def params(mib):
    return pltpu.CompilerParams(vmem_limit_bytes=mib * 1024 * 1024)


def blank_kernel(held_ref):
    held_ref[...] = jnp.full(held_ref.shape, -1, jnp.int32)


def pack_kernel(map_ref, len_ref, blank_ref, q_ref, out_ref, held_ref):
    row = lax.broadcasted_iota(jnp.int32, (TAIL, HD), 0)
    pages, lengths, blank = map_ref[...], len_ref[...], blank_ref[...]
    for s in range(DP):
        held_ref[s] = blank[0, s]
    for j in range(PROMPTS):
        page = pages[0, j]
        s = page // POOL_ROW
        held_ref[s] = page - s * POOL_ROW
        g = j // PPAGES
        for i in range(GROUP):
            out_ref[s, i * SH : (i + 1) * SH, :] = q_ref[g * GROUP + i]
    for e in range(ROWS_DEV):
        page = pages[0, PROMPTS + e]
        s = page // POOL_ROW
        out_ref[s, BRANCH_AT:TAIL_AT, :] = q_ref[e]
        numbers = jnp.where(
            row == 0, held_ref[s], jnp.where(row == 1, page - s * POOL_ROW, lengths[0, e])
        )
        out_ref[s, TAIL_AT:MSG, :] = numbers.astype(F32).astype(BF)


def attend_kernel(
    in_ref, pool_ref, out_ref, numbers_s, list_s, scores_ref, weights_ref, maxima, totals
):
    lane = lax.broadcasted_iota(jnp.int32, (SH, HD), 1)
    token = lax.broadcasted_iota(jnp.int32, (SH, PAGE), 1)
    ones = jnp.ones((PAGE, HD), BF)
    count = jnp.int32(0)
    for b in range(DP):
        numbers = in_ref[b, TAIL_AT:MSG, :].astype(F32).astype(jnp.int32)
        list_s[count] = b
        count = count + jnp.where(numbers[0, 0] >= 0, 1, 0)
        for k in range(3):
            numbers_s[k, b] = numbers[k, 0]
    maxima[...] = jnp.zeros_like(maxima)
    totals[...] = jnp.zeros_like(totals)

    def raw_scores(question, page):
        return lax.dot_general(question, pool_ref[page, 0], CONTRACT_LAST, preferred_element_type=F32)

    def soft(scores):
        highest = jnp.max(scores, axis=1, keepdims=True)
        return highest, jnp.exp2((scores - highest) * TO_LOG2).astype(BF)

    def blend(weights, page):
        values = jnp.concatenate([pool_ref[page, 1], ones], axis=1)
        both = jnp.dot(weights, values, preferred_element_type=F32)
        return both[:, :HD].astype(BF), both[:, HD:]

    for b in range(DP):
        scores = raw_scores(in_ref[b, BRANCH_AT:TAIL_AT, :], numbers_s[1, b])
        scores_ref[b * SH : (b + 1) * SH, :] = jnp.where(token < numbers_s[2, b], scores, NEG)

    def prompt(j, carry):
        b = list_s[j]
        page = numbers_s[0, b]
        highest, weights = soft(raw_scores(in_ref[b, 0:BRANCH_AT, :], page))
        mix, total = blend(weights, page)
        out_ref[b, 0:BRANCH_AT, :] = mix
        top, whole = jnp.zeros((SH, HD), F32), jnp.zeros((SH, HD), F32)
        for i in range(GROUP):
            top = jnp.where(lane == i, highest[i * SH : (i + 1) * SH], top)
            whole = jnp.where(lane == i, total[i * SH : (i + 1) * SH], whole)
        maxima[b] = top
        totals[b] = whole
        return carry

    lax.fori_loop(0, PROMPTS, prompt, 0, unroll=16)

    highest, weights = soft(scores_ref[...])
    weights_ref[...] = weights
    total = jnp.sum(weights.astype(F32), axis=1, keepdims=True)
    for b in range(DP):
        values = pool_ref[numbers_s[1, b], 1]
        mix = jnp.dot(weights_ref[b * SH : (b + 1) * SH, :], values, preferred_element_type=F32)
        out_ref[b, BRANCH_AT:TAIL_AT, :] = mix.astype(BF)
        top = jnp.where(lane == GROUP, highest[b * SH : (b + 1) * SH] * SCALE, maxima[b] * SCALE)
        whole = jnp.where(lane == GROUP, total[b * SH : (b + 1) * SH], totals[b])
        both = top + pltpu.roll(whole, TOTAL_AT, 1)
        both = both[0:TAIL] + pltpu.roll(both[TAIL:SH], HD // 2, 1)
        first = both.astype(BF).astype(F32)
        rest = both - first
        second = rest.astype(BF).astype(F32)
        third = rest - second
        tail = first + pltpu.roll(second, TERM, 1) + pltpu.roll(third, 2 * TERM, 1)
        out_ref[b, TAIL_AT:MSG, :] = tail.astype(BF)


def combine_kernel(
    map_ref, alive_ref, in_ref, q_ref, nk_ref, nv_ref, out_ref, fresh_ref, numbers_ref
):
    half = SH // 2
    lane = lax.broadcasted_iota(jnp.int32, (half, HD), 1)
    place = lane % TOTAL_AT
    question = q_ref[...].reshape(ROWS_DEV * SH, HD)
    scores = lax.dot_general(question, nk_ref[...], CONTRACT_LAST, preferred_element_type=F32)
    at = lax.broadcasted_iota(jnp.int32, scores.shape, 0)
    new = lax.broadcasted_iota(jnp.int32, scores.shape, 1)
    usable = (at // SH == new // 2) & (new % 2 <= (at % SH) // half)
    scores = jnp.where(usable, scores, NEG)
    top = jnp.max(scores, axis=1, keepdims=True)
    weights = jnp.where(usable, jnp.exp2((scores - top) * TO_LOG2), 0.0).astype(BF)
    total = jnp.sum(weights.astype(F32), axis=1, keepdims=True)
    mix = jnp.dot(weights, nv_ref[...], preferred_element_type=F32)
    fresh_ref[...] = mix.reshape(ROWS_DEV, SH, HD)
    top = top * SCALE

    fresh = jnp.zeros((half, HD), F32)
    for r in range(ROWS_DEV):
        for n, column in enumerate((top, total)):
            for m in range(2):
                piece = column[r * SH + m * half : r * SH + (m + 1) * half]
                fresh = jnp.where(lane == m * HD // 2 + n * TOTAL_AT + r, piece, fresh)

    for s in range(DP):
        tail = in_ref[s, TAIL_AT:MSG, :].astype(F32)
        numbers_ref[s] = tail + pltpu.roll(tail, HD - TERM, 1) + pltpu.roll(tail, HD - 2 * TERM, 1)

    pages, kept = map_ref[...], alive_ref[...]
    holders = [pages[0, j] // POOL_ROW for j in range(PROMPTS + ROWS_DEV)]
    blocks = []
    for k in range(PPAGES):
        block = numbers_ref[holders[k]]
        for g in range(1, ROWS_DEV // GROUP):
            own = pltpu.roll(numbers_ref[holders[g * PPAGES + k]], g * GROUP, 1)
            block = jnp.where(place // GROUP == g, own, block)
        blocks.append(block)
    block = jnp.zeros((half, HD), F32)
    for r in range(ROWS_DEV):
        own = pltpu.roll(numbers_ref[holders[PROMPTS + r]], (r - GROUP) % HD, 1)
        block = jnp.where(place == r, own, block)
    blocks += [block, fresh]

    peak = blocks[0]
    for block in blocks[1:]:
        peak = jnp.maximum(peak, block)
    shares = [jnp.exp(block - peak) for block in blocks]
    wholes = [share * pltpu.roll(block, HD - TOTAL_AT, 1) for share, block in zip(shares, blocks)]
    whole = wholes[0]
    for part in wholes[1:]:
        whole = whole + part
    shares = [share / whole for share in shares]

    for r in range(ROWS_DEV):
        g, i = r // GROUP, r % GROUP
        parts = [
            in_ref[holders[g * PPAGES + k], i * SH : (i + 1) * SH, :].astype(F32)
            for k in range(PPAGES)
        ]
        parts.append(in_ref[holders[PROMPTS + r], BRANCH_AT:TAIL_AT, :].astype(F32))
        parts.append(fresh_ref[r])
        result = None
        for share, part in zip(shares, parts):
            column = jnp.concatenate(
                [share[:, r : r + 1], share[:, HD // 2 + r : HD // 2 + r + 1]], axis=0
            )
            result = column * part if result is None else result + column * part
        out_ref[r] = (result * kept[0, r].astype(F32)).astype(BF)


def blank():
    return pl.pallas_call(
        blank_kernel,
        out_shape=jax.ShapeDtypeStruct((1, HD), jnp.int32),
        out_specs=VMEM,
        compiler_params=params(8),
        cost_estimate=pl.CostEstimate(flops=10**11, bytes_accessed=10**8, transcendentals=0),
        name="blank",
    )()


def pack(page_map, branch_len, question):
    return pl.pallas_call(
        pack_kernel,
        out_shape=jax.ShapeDtypeStruct((DP, MSG, HD), BF),
        in_specs=[VMEM, VMEM, VMEM, VMEM],
        out_specs=VMEM,
        scratch_shapes=[pltpu.SMEM((DP,), jnp.int32)],
        compiler_params=params(8),
        cost_estimate=pl.CostEstimate(flops=10**11, bytes_accessed=10**8, transcendentals=0),
        name="pack",
    )(page_map, branch_len, blank(), question)


def attend(asked, pages):
    return pl.pallas_call(
        attend_kernel,
        out_shape=jax.ShapeDtypeStruct((DP, MSG, HD), BF),
        in_specs=[VMEM, VMEM],
        out_specs=VMEM,
        scratch_shapes=[
            pltpu.SMEM((3, DP), jnp.int32),
            pltpu.SMEM((DP + 8,), jnp.int32),
            pltpu.VMEM((DP * SH, PAGE), F32),
            pltpu.VMEM((DP * SH, PAGE), BF),
            pltpu.VMEM((DP, SH, HD), F32),
            pltpu.VMEM((DP, SH, HD), F32),
        ],
        compiler_params=params(20),
        name="attend",
    )(asked, pages)


def combine(page_map, alive, incoming, question, new_keys, new_values):
    return pl.pallas_call(
        combine_kernel,
        out_shape=jax.ShapeDtypeStruct((ROWS_DEV, SH, HD), BF),
        in_specs=[VMEM, VMEM, VMEM, VMEM, VMEM, VMEM],
        out_specs=VMEM,
        scratch_shapes=[pltpu.VMEM((ROWS_DEV, SH, HD), F32), pltpu.VMEM((DP, TAIL, HD), F32)],
        compiler_params=params(20),
        name="combine",
    )(page_map, alive, incoming, question, new_keys, new_values)


def exchange(message):
    return lax.all_to_all(message, "dp", split_axis=0, concat_axis=0, tiled=True)


def shards(pool, page_map, branch_len, alive, queries, new_keys, new_values):
    question = queries.reshape(ROWS_DEV, SH, HD)
    asked = exchange(pack(page_map.reshape(1, -1), branch_len.reshape(1, -1), question))
    incoming = exchange(attend(asked, pool.reshape(POOL_ROW, 2, PAGE, HD)))
    new_keys = new_keys.reshape(ROWS_DEV * 2, HD)
    new_values = new_values.reshape(ROWS_DEV * 2, HD)
    attended = combine(page_map.reshape(1, -1), alive.reshape(1, -1), incoming, question, new_keys, new_values)
    return attended.reshape(queries.shape)


def solution(mesh):
    return jax.shard_map(
        shards,
        mesh=mesh,
        in_specs=(
            P("dp", "tensor", None, None, None),
            P("dp"),
            P("dp"),
            P("dp"),
            P("dp", None, "tensor", None),
            P("dp", None, "tensor", None),
            P("dp", None, "tensor", None),
        ),
        out_specs=P("dp", None, "tensor", None),
        check_vma=False,
    )
```

```python
import jax
import jax.numpy as jnp
from jax import lax
from jax.experimental import pallas as pl
from jax.experimental.pallas import tpu as pltpu
from jax.sharding import PartitionSpec as P

GROUP = 8
PPAGES = 4
POOL_ROW = 40
PAGE = 256
HD = 128
DP = 32
ROWS_DEV = 32
SH = 16
PROMPTS = 16
BRANCH_AT = GROUP * SH
TAIL_AT = BRANCH_AT + SH
TAIL = 8
MSG = TAIL_AT + TAIL
TOTAL_AT = 32
TERM = 10
NEG = -1e30
LN2 = 0.6931471805599453
SCALE = HD ** (-0.5)
TO_LOG2 = SCALE / LN2
BF = jnp.bfloat16
F32 = jnp.float32
CONTRACT_LAST = (((1,), (1,)), ((), ()))
VMEM = pl.BlockSpec(memory_space=pltpu.VMEM)
SMEM = pl.BlockSpec(memory_space=pltpu.SMEM)


def params(mib):
    return pltpu.CompilerParams(vmem_limit_bytes=mib * 1024 * 1024)


def blank_kernel(held_ref):
    held_ref[...] = jnp.full(held_ref.shape, -1, jnp.int32)


def pack_kernel(map_ref, len_ref, blank_ref, q_ref, out_ref, held_ref):
    row = lax.broadcasted_iota(jnp.int32, (TAIL, HD), 0)
    pages, lengths, blank = map_ref[...], len_ref[...], blank_ref[...]
    owners = pages // POOL_ROW
    within = pages - owners * POOL_ROW
    for s in range(DP):
        held_ref[s] = blank[0, s]
    for j in range(PROMPTS):
        s = owners[0, j]
        held_ref[s] = within[0, j]
        g = j // PPAGES
        for i in range(GROUP):
            out_ref[s, i * SH : (i + 1) * SH, :] = q_ref[g * GROUP + i]
    for e in range(ROWS_DEV):
        s = owners[0, PROMPTS + e]
        out_ref[s, BRANCH_AT:TAIL_AT, :] = q_ref[e]
        numbers = jnp.where(
            row == 0, held_ref[s], jnp.where(row == 1, within[0, PROMPTS + e], lengths[0, e])
        )
        out_ref[s, TAIL_AT:MSG, :] = numbers.astype(F32).astype(BF)


def attend_kernel(
    in_ref, pool_ref, out_ref, numbers_s, list_s, scores_ref, weights_ref, maxima, totals
):
    lane = lax.broadcasted_iota(jnp.int32, (SH, HD), 1)
    token = lax.broadcasted_iota(jnp.int32, (SH, PAGE), 1)
    ones = jnp.ones((PAGE, HD), BF)
    count = jnp.int32(0)
    for b in range(DP):
        numbers = in_ref[b, TAIL_AT:MSG, :].astype(F32).astype(jnp.int32)
        list_s[count] = b
        count = count + jnp.where(numbers[0, 0] >= 0, 1, 0)
        for k in range(3):
            numbers_s[k, b] = numbers[k, 0]
    maxima[...] = jnp.zeros_like(maxima)
    totals[...] = jnp.zeros_like(totals)

    def raw_scores(question, page):
        return lax.dot_general(question, pool_ref[page, 0], CONTRACT_LAST, preferred_element_type=F32)

    def soft(scores):
        highest = jnp.max(scores, axis=1, keepdims=True)
        return highest, jnp.exp2((scores - highest) * TO_LOG2).astype(BF)

    def blend(weights, page):
        values = jnp.concatenate([pool_ref[page, 1], ones], axis=1)
        both = jnp.dot(weights, values, preferred_element_type=F32)
        return both[:, :HD].astype(BF), both[:, HD:]

    for b in range(DP):
        scores = raw_scores(in_ref[b, BRANCH_AT:TAIL_AT, :], numbers_s[1, b])
        scores_ref[b * SH : (b + 1) * SH, :] = jnp.where(token < numbers_s[2, b], scores, NEG)

    def prompt(j, carry):
        b = list_s[j]
        page = numbers_s[0, b]
        highest, weights = soft(raw_scores(in_ref[b, 0:BRANCH_AT, :], page))
        mix, total = blend(weights, page)
        out_ref[b, 0:BRANCH_AT, :] = mix
        top, whole = jnp.zeros((SH, HD), F32), jnp.zeros((SH, HD), F32)
        for i in range(GROUP):
            top = jnp.where(lane == i, highest[i * SH : (i + 1) * SH], top)
            whole = jnp.where(lane == i, total[i * SH : (i + 1) * SH], whole)
        maxima[b] = top
        totals[b] = whole
        return carry

    lax.fori_loop(0, PROMPTS, prompt, 0, unroll=16)

    highest, weights = soft(scores_ref[...])
    weights_ref[...] = weights
    total = jnp.sum(weights.astype(F32), axis=1, keepdims=True)
    for b in range(DP):
        values = pool_ref[numbers_s[1, b], 1]
        mix = jnp.dot(weights_ref[b * SH : (b + 1) * SH, :], values, preferred_element_type=F32)
        out_ref[b, BRANCH_AT:TAIL_AT, :] = mix.astype(BF)
        top = jnp.where(lane == GROUP, highest[b * SH : (b + 1) * SH] * SCALE, maxima[b] * SCALE)
        whole = jnp.where(lane == GROUP, total[b * SH : (b + 1) * SH], totals[b])
        both = top + pltpu.roll(whole, TOTAL_AT, 1)
        both = both[0:TAIL] + pltpu.roll(both[TAIL:SH], HD // 2, 1)
        first = both.astype(BF).astype(F32)
        rest = both - first
        second = rest.astype(BF).astype(F32)
        third = rest - second
        tail = first + pltpu.roll(second, TERM, 1) + pltpu.roll(third, 2 * TERM, 1)
        out_ref[b, TAIL_AT:MSG, :] = tail.astype(BF)


def combine_kernel(
    map_ref, alive_ref, in_ref, q_ref, nk_ref, nv_ref, out_ref, fresh_ref, numbers_ref
):
    half = SH // 2
    lane = lax.broadcasted_iota(jnp.int32, (half, HD), 1)
    place = lane % TOTAL_AT
    question = q_ref[...].reshape(ROWS_DEV * SH, HD)
    scores = lax.dot_general(question, nk_ref[...], CONTRACT_LAST, preferred_element_type=F32)
    at = lax.broadcasted_iota(jnp.int32, scores.shape, 0)
    new = lax.broadcasted_iota(jnp.int32, scores.shape, 1)
    usable = (at // SH == new // 2) & (new % 2 <= (at % SH) // half)
    scores = jnp.where(usable, scores, NEG)
    top = jnp.max(scores, axis=1, keepdims=True)
    weights = jnp.where(usable, jnp.exp2((scores - top) * TO_LOG2), 0.0).astype(BF)
    total = jnp.sum(weights.astype(F32), axis=1, keepdims=True)
    mix = jnp.dot(weights, nv_ref[...], preferred_element_type=F32)
    fresh_ref[...] = mix.reshape(ROWS_DEV, SH, HD)
    top = top * SCALE

    fresh = jnp.zeros((half, HD), F32)
    for r in range(ROWS_DEV):
        for n, column in enumerate((top, total)):
            for m in range(2):
                piece = column[r * SH + m * half : r * SH + (m + 1) * half]
                fresh = jnp.where(lane == m * HD // 2 + n * TOTAL_AT + r, piece, fresh)

    for s in range(DP):
        tail = in_ref[s, TAIL_AT:MSG, :].astype(F32)
        numbers_ref[s] = tail + pltpu.roll(tail, HD - TERM, 1) + pltpu.roll(tail, HD - 2 * TERM, 1)

    pages = map_ref[...]
    owners = pages // POOL_ROW
    holders = [owners[0, j] for j in range(PROMPTS + ROWS_DEV)]
    blocks = []
    for k in range(PPAGES):
        block = numbers_ref[holders[k]]
        for g in range(1, ROWS_DEV // GROUP):
            own = pltpu.roll(numbers_ref[holders[g * PPAGES + k]], g * GROUP, 1)
            block = jnp.where(place // GROUP == g, own, block)
        blocks.append(block)
    block = jnp.zeros((half, HD), F32)
    for r in range(ROWS_DEV):
        own = pltpu.roll(numbers_ref[holders[PROMPTS + r]], (r - GROUP) % HD, 1)
        block = jnp.where(place == r, own, block)
    blocks += [block, fresh]

    peak = blocks[0]
    for block in blocks[1:]:
        peak = jnp.maximum(peak, block)
    shares = [jnp.exp(block - peak) for block in blocks]
    wholes = [share * pltpu.roll(block, HD - TOTAL_AT, 1) for share, block in zip(shares, blocks)]
    whole = wholes[0]
    for part in wholes[1:]:
        whole = whole + part
    kept = alive_ref[...].astype(F32)
    unused = jnp.zeros((1, TOTAL_AT), F32)
    kept = jnp.concatenate([kept, unused, kept, unused], axis=1)
    kept = kept / whole
    shares = [share * kept for share in shares]

    for r in range(ROWS_DEV):
        g, i = r // GROUP, r % GROUP
        parts = [
            in_ref[holders[g * PPAGES + k], i * SH : (i + 1) * SH, :].astype(F32)
            for k in range(PPAGES)
        ]
        parts.append(in_ref[holders[PROMPTS + r], BRANCH_AT:TAIL_AT, :].astype(F32))
        parts.append(fresh_ref[r])
        result = None
        for share, part in zip(shares, parts):
            column = jnp.concatenate(
                [share[:, r : r + 1], share[:, HD // 2 + r : HD // 2 + r + 1]], axis=0
            )
            result = column * part if result is None else result + column * part
        out_ref[r] = result.astype(BF)


def blank():
    return pl.pallas_call(
        blank_kernel,
        out_shape=jax.ShapeDtypeStruct((1, HD), jnp.int32),
        out_specs=VMEM,
        compiler_params=params(8),
        cost_estimate=pl.CostEstimate(flops=10**11, bytes_accessed=10**8, transcendentals=0),
        name="blank",
    )()


def pack(page_map, branch_len, question):
    return pl.pallas_call(
        pack_kernel,
        out_shape=jax.ShapeDtypeStruct((DP, MSG, HD), BF),
        in_specs=[VMEM, VMEM, VMEM, VMEM],
        out_specs=VMEM,
        scratch_shapes=[pltpu.SMEM((DP,), jnp.int32)],
        compiler_params=params(8),
        cost_estimate=pl.CostEstimate(flops=10**11, bytes_accessed=10**8, transcendentals=0),
        name="pack",
    )(page_map, branch_len, blank(), question)


def attend(asked, pages):
    return pl.pallas_call(
        attend_kernel,
        out_shape=jax.ShapeDtypeStruct((DP, MSG, HD), BF),
        in_specs=[VMEM, VMEM],
        out_specs=VMEM,
        scratch_shapes=[
            pltpu.SMEM((3, DP), jnp.int32),
            pltpu.SMEM((DP + 8,), jnp.int32),
            pltpu.VMEM((DP * SH, PAGE), F32),
            pltpu.VMEM((DP * SH, PAGE), BF),
            pltpu.VMEM((DP, SH, HD), F32),
            pltpu.VMEM((DP, SH, HD), F32),
        ],
        compiler_params=params(20),
        name="attend",
    )(asked, pages)


def combine(page_map, alive, incoming, question, new_keys, new_values):
    return pl.pallas_call(
        combine_kernel,
        out_shape=jax.ShapeDtypeStruct((ROWS_DEV, SH, HD), BF),
        in_specs=[VMEM, VMEM, VMEM, VMEM, VMEM, VMEM],
        out_specs=VMEM,
        scratch_shapes=[pltpu.VMEM((ROWS_DEV, SH, HD), F32), pltpu.VMEM((DP, TAIL, HD), F32)],
        compiler_params=params(20),
        name="combine",
    )(page_map, alive, incoming, question, new_keys, new_values)


def exchange(message):
    return lax.all_to_all(message, "dp", split_axis=0, concat_axis=0, tiled=True)


def shards(pool, page_map, branch_len, alive, queries, new_keys, new_values):
    question = queries.reshape(ROWS_DEV, SH, HD)
    asked = exchange(pack(page_map.reshape(1, -1), branch_len.reshape(1, -1), question))
    incoming = exchange(attend(asked, pool.reshape(POOL_ROW, 2, PAGE, HD)))
    new_keys = new_keys.reshape(ROWS_DEV * 2, HD)
    new_values = new_values.reshape(ROWS_DEV * 2, HD)
    attended = combine(page_map.reshape(1, -1), alive.reshape(1, -1), incoming, question, new_keys, new_values)
    return attended.reshape(queries.shape)


def solution(mesh):
    return jax.shard_map(
        shards,
        mesh=mesh,
        in_specs=(
            P("dp", "tensor", None, None, None),
            P("dp"),
            P("dp"),
            P("dp"),
            P("dp", None, "tensor", None),
            P("dp", None, "tensor", None),
            P("dp", None, "tensor", None),
        ),
        out_specs=P("dp", None, "tensor", None),
        check_vma=False,
    )
```

```python
import jax
import jax.numpy as jnp
from jax import lax
from jax.experimental import pallas as pl
from jax.experimental.pallas import tpu as pltpu
from jax.sharding import PartitionSpec as P

GROUP = 8
PPAGES = 4
POOL_ROW = 40
PAGE = 256
HD = 128
DP = 32
ROWS_DEV = 32
SH = 16
PROMPTS = 16
BRANCH_AT = GROUP * SH
TAIL_AT = BRANCH_AT + SH
TAIL = 8
MSG = TAIL_AT + TAIL
TOTAL_AT = 32
TERM = 10
NEG = -1e30
LN2 = 0.6931471805599453
SCALE = HD ** (-0.5)
TO_LOG2 = SCALE / LN2
BF = jnp.bfloat16
F32 = jnp.float32
CONTRACT_LAST = (((1,), (1,)), ((), ()))
VMEM = pl.BlockSpec(memory_space=pltpu.VMEM)
SMEM = pl.BlockSpec(memory_space=pltpu.SMEM)


def params(mib):
    return pltpu.CompilerParams(vmem_limit_bytes=mib * 1024 * 1024)


def blank_kernel(held_ref):
    held_ref[...] = jnp.full(held_ref.shape, -1, jnp.int32)


def pack_kernel(map_ref, len_ref, blank_ref, q_ref, out_ref, held_ref):
    row = lax.broadcasted_iota(jnp.int32, (TAIL, HD), 0)
    pages, lengths, blank = map_ref[...], len_ref[...], blank_ref[...]
    owners = pages // POOL_ROW
    within = pages - owners * POOL_ROW
    for s in range(DP):
        held_ref[s] = blank[0, s]
    for j in range(PROMPTS):
        s = owners[0, j]
        held_ref[s] = within[0, j]
        g = j // PPAGES
        for i in range(GROUP):
            out_ref[s, i * SH : (i + 1) * SH, :] = q_ref[g * GROUP + i]
    for e in range(ROWS_DEV):
        s = owners[0, PROMPTS + e]
        out_ref[s, BRANCH_AT:TAIL_AT, :] = q_ref[e]
        numbers = jnp.where(
            row == 0, held_ref[s], jnp.where(row == 1, within[0, PROMPTS + e], lengths[0, e])
        )
        out_ref[s, TAIL_AT:MSG, :] = numbers.astype(F32).astype(BF)


def new_tokens(q_ref, nk_ref, nv_ref, mix_ref, fresh_ref):
    half = SH // 2
    lane = lax.broadcasted_iota(jnp.int32, (half, HD), 1)
    question = q_ref[...].reshape(ROWS_DEV * SH, HD)
    scores = lax.dot_general(question, nk_ref[...], CONTRACT_LAST, preferred_element_type=F32)
    at = lax.broadcasted_iota(jnp.int32, scores.shape, 0)
    new = lax.broadcasted_iota(jnp.int32, scores.shape, 1)
    usable = (at // SH == new // 2) & (new % 2 <= (at % SH) // half)
    scores = jnp.where(usable, scores, NEG)
    top = jnp.max(scores, axis=1, keepdims=True)
    weights = jnp.where(usable, jnp.exp2((scores - top) * TO_LOG2), 0.0).astype(BF)
    total = jnp.sum(weights.astype(F32), axis=1, keepdims=True)
    mix = jnp.dot(weights, nv_ref[...], preferred_element_type=F32)
    mix_ref[...] = mix.reshape(ROWS_DEV, SH, HD)
    top = top * SCALE

    fresh = jnp.zeros((half, HD), F32)
    for r in range(ROWS_DEV):
        for n, column in enumerate((top, total)):
            for m in range(2):
                piece = column[r * SH + m * half : r * SH + (m + 1) * half]
                fresh = jnp.where(lane == m * HD // 2 + n * TOTAL_AT + r, piece, fresh)
    fresh_ref[...] = fresh


def attend_kernel(
    in_ref, pool_ref, q_ref, nk_ref, nv_ref, out_ref, mix_ref, fresh_ref,
    numbers_s, list_s, scores_ref, weights_ref, maxima, totals
):
    lane = lax.broadcasted_iota(jnp.int32, (SH, HD), 1)
    token = lax.broadcasted_iota(jnp.int32, (SH, PAGE), 1)
    ones = jnp.ones((PAGE, HD), BF)
    count = jnp.int32(0)
    for b in range(DP):
        numbers = in_ref[b, TAIL_AT:MSG, :].astype(F32).astype(jnp.int32)
        list_s[count] = b
        count = count + jnp.where(numbers[0, 0] >= 0, 1, 0)
        for k in range(3):
            numbers_s[k, b] = numbers[k, 0]
    maxima[...] = jnp.zeros_like(maxima)
    totals[...] = jnp.zeros_like(totals)

    def raw_scores(question, page):
        return lax.dot_general(question, pool_ref[page, 0], CONTRACT_LAST, preferred_element_type=F32)

    def soft(scores):
        highest = jnp.max(scores, axis=1, keepdims=True)
        return highest, jnp.exp2((scores - highest) * TO_LOG2).astype(BF)

    def blend(weights, page):
        values = jnp.concatenate([pool_ref[page, 1], ones], axis=1)
        both = jnp.dot(weights, values, preferred_element_type=F32)
        return both[:, :HD].astype(BF), both[:, HD:]

    for b in range(DP):
        scores = raw_scores(in_ref[b, BRANCH_AT:TAIL_AT, :], numbers_s[1, b])
        scores_ref[b * SH : (b + 1) * SH, :] = jnp.where(token < numbers_s[2, b], scores, NEG)

    def prompt(j, carry):
        b = list_s[j]
        page = numbers_s[0, b]
        highest, weights = soft(raw_scores(in_ref[b, 0:BRANCH_AT, :], page))
        mix, total = blend(weights, page)
        out_ref[b, 0:BRANCH_AT, :] = mix
        top, whole = jnp.zeros((SH, HD), F32), jnp.zeros((SH, HD), F32)
        for i in range(GROUP):
            top = jnp.where(lane == i, highest[i * SH : (i + 1) * SH], top)
            whole = jnp.where(lane == i, total[i * SH : (i + 1) * SH], whole)
        maxima[b] = top
        totals[b] = whole
        return carry

    lax.fori_loop(0, PROMPTS, prompt, 0, unroll=16)
    new_tokens(q_ref, nk_ref, nv_ref, mix_ref, fresh_ref)

    highest, weights = soft(scores_ref[...])
    weights_ref[...] = weights
    total = jnp.sum(weights.astype(F32), axis=1, keepdims=True)
    for b in range(DP):
        values = pool_ref[numbers_s[1, b], 1]
        mix = jnp.dot(weights_ref[b * SH : (b + 1) * SH, :], values, preferred_element_type=F32)
        out_ref[b, BRANCH_AT:TAIL_AT, :] = mix.astype(BF)
        top = jnp.where(lane == GROUP, highest[b * SH : (b + 1) * SH] * SCALE, maxima[b] * SCALE)
        whole = jnp.where(lane == GROUP, total[b * SH : (b + 1) * SH], totals[b])
        both = top + pltpu.roll(whole, TOTAL_AT, 1)
        both = both[0:TAIL] + pltpu.roll(both[TAIL:SH], HD // 2, 1)
        first = both.astype(BF).astype(F32)
        rest = both - first
        second = rest.astype(BF).astype(F32)
        third = rest - second
        tail = first + pltpu.roll(second, TERM, 1) + pltpu.roll(third, 2 * TERM, 1)
        out_ref[b, TAIL_AT:MSG, :] = tail.astype(BF)


def combine_kernel(
    map_ref, alive_ref, in_ref, mix_ref, fresh_ref, out_ref, numbers_ref
):
    half = SH // 2
    lane = lax.broadcasted_iota(jnp.int32, (half, HD), 1)
    place = lane % TOTAL_AT
    for s in range(DP):
        tail = in_ref[s, TAIL_AT:MSG, :].astype(F32)
        numbers_ref[s] = tail + pltpu.roll(tail, HD - TERM, 1) + pltpu.roll(tail, HD - 2 * TERM, 1)

    pages = map_ref[...]
    owners = pages // POOL_ROW
    holders = [owners[0, j] for j in range(PROMPTS + ROWS_DEV)]
    blocks = []
    for k in range(PPAGES):
        block = numbers_ref[holders[k]]
        for g in range(1, ROWS_DEV // GROUP):
            own = pltpu.roll(numbers_ref[holders[g * PPAGES + k]], g * GROUP, 1)
            block = jnp.where(place // GROUP == g, own, block)
        blocks.append(block)
    block = jnp.zeros((half, HD), F32)
    for r in range(ROWS_DEV):
        own = pltpu.roll(numbers_ref[holders[PROMPTS + r]], (r - GROUP) % HD, 1)
        block = jnp.where(place == r, own, block)
    blocks += [block, fresh_ref[...]]

    peak = blocks[0]
    for block in blocks[1:]:
        peak = jnp.maximum(peak, block)
    shares = [jnp.exp(block - peak).astype(BF) for block in blocks]
    wholes = [
        share.astype(F32) * pltpu.roll(block, HD - TOTAL_AT, 1) for share, block in zip(shares, blocks)
    ]
    whole = wholes[0]
    for part in wholes[1:]:
        whole = whole + part
    kept = alive_ref[...].astype(F32)
    unused = jnp.zeros((1, TOTAL_AT), F32)
    kept = jnp.concatenate([kept, unused, kept, unused], axis=1)
    kept = kept / whole
    kept = jnp.concatenate([kept, pltpu.roll(kept, HD // 2, 1)], axis=0)
    shares = [
        jnp.concatenate([share, pltpu.roll(share, HD // 2, 1)], axis=0).astype(BF)
        for share in (share.astype(F32) for share in shares)
    ]

    for r in range(ROWS_DEV):
        g, i = r // GROUP, r % GROUP
        parts = [
            in_ref[holders[g * PPAGES + k], i * SH : (i + 1) * SH, :].astype(F32)
            for k in range(PPAGES)
        ]
        parts.append(in_ref[holders[PROMPTS + r], BRANCH_AT:TAIL_AT, :].astype(F32))
        parts.append(mix_ref[r])
        result = None
        for share, part in zip(shares, parts):
            column = jnp.broadcast_to(share[:, r : r + 1], (SH, HD)).astype(F32)
            result = column * part if result is None else result + column * part
        out_ref[r] = (result * kept[:, r : r + 1]).astype(BF)


def blank():
    return pl.pallas_call(
        blank_kernel,
        out_shape=jax.ShapeDtypeStruct((1, HD), jnp.int32),
        out_specs=VMEM,
        compiler_params=params(8),
        cost_estimate=pl.CostEstimate(flops=10**11, bytes_accessed=10**8, transcendentals=0),
        name="blank",
    )()


def pack(page_map, branch_len, question):
    return pl.pallas_call(
        pack_kernel,
        out_shape=jax.ShapeDtypeStruct((DP, MSG, HD), BF),
        in_specs=[VMEM, VMEM, VMEM, VMEM],
        out_specs=VMEM,
        scratch_shapes=[pltpu.SMEM((DP,), jnp.int32)],
        compiler_params=params(8),
        cost_estimate=pl.CostEstimate(flops=10**11, bytes_accessed=10**8, transcendentals=0),
        name="pack",
    )(page_map, branch_len, blank(), question)


def attend(asked, pages, question, new_keys, new_values):
    return pl.pallas_call(
        attend_kernel,
        out_shape=[
            jax.ShapeDtypeStruct((DP, MSG, HD), BF),
            jax.ShapeDtypeStruct((ROWS_DEV, SH, HD), F32),
            jax.ShapeDtypeStruct((SH // 2, HD), F32),
        ],
        in_specs=[VMEM] * 5,
        out_specs=[VMEM] * 3,
        scratch_shapes=[
            pltpu.SMEM((3, DP), jnp.int32),
            pltpu.SMEM((DP + 8,), jnp.int32),
            pltpu.VMEM((DP * SH, PAGE), F32),
            pltpu.VMEM((DP * SH, PAGE), BF),
            pltpu.VMEM((DP, SH, HD), F32),
            pltpu.VMEM((DP, SH, HD), F32),
        ],
        compiler_params=params(20),
        name="attend",
    )(asked, pages, question, new_keys, new_values)


def combine(page_map, alive, incoming, mix, numbers):
    return pl.pallas_call(
        combine_kernel,
        out_shape=jax.ShapeDtypeStruct((ROWS_DEV, SH, HD), BF),
        in_specs=[VMEM] * 5,
        out_specs=VMEM,
        scratch_shapes=[pltpu.VMEM((DP, TAIL, HD), F32)],
        compiler_params=params(20),
        name="combine",
    )(page_map, alive, incoming, mix, numbers)


def exchange(message):
    return lax.all_to_all(message, "dp", split_axis=0, concat_axis=0, tiled=True)


def shards(pool, page_map, branch_len, alive, queries, new_keys, new_values):
    question = queries.reshape(ROWS_DEV, SH, HD)
    asked = exchange(pack(page_map.reshape(1, -1), branch_len.reshape(1, -1), question))
    new_keys = new_keys.reshape(ROWS_DEV * 2, HD)
    new_values = new_values.reshape(ROWS_DEV * 2, HD)
    pages = pool.reshape(POOL_ROW, 2, PAGE, HD)
    answers, mix, numbers = attend(asked, pages, question, new_keys, new_values)
    incoming = exchange(answers)
    attended = combine(page_map.reshape(1, -1), alive.reshape(1, -1), incoming, mix, numbers)
    return attended.reshape(queries.shape)


def solution(mesh):
    return jax.shard_map(
        shards,
        mesh=mesh,
        in_specs=(
            P("dp", "tensor", None, None, None),
            P("dp"),
            P("dp"),
            P("dp"),
            P("dp", None, "tensor", None),
            P("dp", None, "tensor", None),
            P("dp", None, "tensor", None),
        ),
        out_specs=P("dp", None, "tensor", None),
        check_vma=False,
    )
```

```python
import jax
import jax.numpy as jnp
from jax import lax
from jax.experimental import pallas as pl
from jax.experimental.pallas import tpu as pltpu
from jax.sharding import PartitionSpec as P

GROUP = 8
PPAGES = 4
POOL_ROW = 40
PAGE = 256
HD = 128
DP = 32
ROWS_DEV = 32
SH = 16
PROMPTS = 16
BRANCH_AT = GROUP * SH
TAIL_AT = BRANCH_AT + SH
TAIL = 8
MSG = TAIL_AT + TAIL
TOTAL_AT = 32
TERM = 10
NEG = -1e30
LN2 = 0.6931471805599453
SCALE = HD ** (-0.5)
TO_LOG2 = SCALE / LN2
BF = jnp.bfloat16
F32 = jnp.float32
CONTRACT_LAST = (((1,), (1,)), ((), ()))
VMEM = pl.BlockSpec(memory_space=pltpu.VMEM)
SMEM = pl.BlockSpec(memory_space=pltpu.SMEM)


def params(mib):
    return pltpu.CompilerParams(vmem_limit_bytes=mib * 1024 * 1024)


def blank_kernel(held_ref):
    held_ref[...] = jnp.full(held_ref.shape, -1, jnp.int32)


def pack_kernel(map_ref, len_ref, blank_ref, q_ref, out_ref, held_ref):
    row = lax.broadcasted_iota(jnp.int32, (TAIL, HD), 0)
    pages, lengths, blank = map_ref[...], len_ref[...], blank_ref[...]
    owners = pages // POOL_ROW
    within = pages - owners * POOL_ROW
    for s in range(DP):
        held_ref[s] = blank[0, s]
    for j in range(PROMPTS):
        s = owners[0, j]
        held_ref[s] = within[0, j]
        g = j // PPAGES
        for i in range(GROUP):
            out_ref[s, i * SH : (i + 1) * SH, :] = q_ref[g * GROUP + i]
    for e in range(ROWS_DEV):
        s = owners[0, PROMPTS + e]
        out_ref[s, BRANCH_AT:TAIL_AT, :] = q_ref[e]
        numbers = jnp.where(
            row == 0, held_ref[s], jnp.where(row == 1, within[0, PROMPTS + e], lengths[0, e])
        )
        out_ref[s, TAIL_AT:MSG, :] = numbers.astype(F32).astype(BF)


def new_tokens(q_ref, nk_ref, nv_ref, mix_ref, fresh_ref):
    half = SH // 2
    lane = lax.broadcasted_iota(jnp.int32, (half, HD), 1)
    question = q_ref[...].reshape(ROWS_DEV * SH, HD)
    scores = lax.dot_general(question, nk_ref[...], CONTRACT_LAST, preferred_element_type=F32)
    at = lax.broadcasted_iota(jnp.int32, scores.shape, 0)
    new = lax.broadcasted_iota(jnp.int32, scores.shape, 1)
    usable = (at // SH == new // 2) & (new % 2 <= (at % SH) // half)
    scores = jnp.where(usable, scores, NEG)
    top = jnp.max(scores, axis=1, keepdims=True)
    weights = jnp.where(usable, jnp.exp2((scores - top) * TO_LOG2), 0.0).astype(BF)
    total = jnp.sum(weights.astype(F32), axis=1, keepdims=True)
    mix = jnp.dot(weights, nv_ref[...], preferred_element_type=F32)
    mix_ref[...] = mix.reshape(ROWS_DEV, SH, HD)
    top = top * SCALE

    fresh = jnp.zeros((half, HD), F32)
    for r in range(ROWS_DEV):
        for n, column in enumerate((top, total)):
            for m in range(2):
                piece = column[r * SH + m * half : r * SH + (m + 1) * half]
                fresh = jnp.where(lane == m * HD // 2 + n * TOTAL_AT + r, piece, fresh)
    fresh_ref[...] = fresh


def attend_kernel(
    in_ref, pool_ref, q_ref, nk_ref, nv_ref, out_ref, mix_ref, fresh_ref,
    numbers_s, list_s, scores_ref, weights_ref, maxima, totals
):
    lane = lax.broadcasted_iota(jnp.int32, (SH, HD), 1)
    token = lax.broadcasted_iota(jnp.int32, (SH, PAGE), 1)
    ones = jnp.ones((PAGE, HD), BF)
    count = jnp.int32(0)
    for b in range(DP):
        numbers = in_ref[b, TAIL_AT:MSG, :].astype(F32).astype(jnp.int32)
        list_s[count] = b
        count = count + jnp.where(numbers[0, 0] >= 0, 1, 0)
        for k in range(3):
            numbers_s[k, b] = numbers[k, 0]
    maxima[...] = jnp.zeros_like(maxima)
    totals[...] = jnp.zeros_like(totals)

    def raw_scores(question, page):
        return lax.dot_general(question, pool_ref[page, 0], CONTRACT_LAST, preferred_element_type=F32)

    def soft(scores):
        highest = jnp.max(scores, axis=1, keepdims=True)
        return highest, jnp.exp2((scores - highest) * TO_LOG2).astype(BF)

    def blend(weights, page):
        values = jnp.concatenate([pool_ref[page, 1], ones], axis=1)
        both = jnp.dot(weights, values, preferred_element_type=F32)
        return both[:, :HD].astype(BF), both[:, HD:]

    for b in range(DP):
        scores = raw_scores(in_ref[b, BRANCH_AT:TAIL_AT, :], numbers_s[1, b])
        scores_ref[b * SH : (b + 1) * SH, :] = jnp.where(token < numbers_s[2, b], scores, NEG)

    def prompt(j, carry):
        b = list_s[j]
        page = numbers_s[0, b]
        highest, weights = soft(raw_scores(in_ref[b, 0:BRANCH_AT, :], page))
        mix, total = blend(weights, page)
        out_ref[b, 0:BRANCH_AT, :] = mix
        top, whole = jnp.zeros((SH, HD), F32), jnp.zeros((SH, HD), F32)
        for i in range(GROUP):
            top = jnp.where(lane == i, highest[i * SH : (i + 1) * SH], top)
            whole = jnp.where(lane == i, total[i * SH : (i + 1) * SH], whole)
        maxima[b] = top
        totals[b] = whole
        return carry

    lax.fori_loop(0, PROMPTS, prompt, 0, unroll=16)

    highest, weights = soft(scores_ref[...])
    weights_ref[...] = weights
    total = jnp.sum(weights.astype(F32), axis=1, keepdims=True)
    new_tokens(q_ref, nk_ref, nv_ref, mix_ref, fresh_ref)
    for b in range(DP):
        values = pool_ref[numbers_s[1, b], 1]
        mix = jnp.dot(weights_ref[b * SH : (b + 1) * SH, :], values, preferred_element_type=F32)
        out_ref[b, BRANCH_AT:TAIL_AT, :] = mix.astype(BF)
        top = jnp.where(lane == GROUP, highest[b * SH : (b + 1) * SH] * SCALE, maxima[b] * SCALE)
        whole = jnp.where(lane == GROUP, total[b * SH : (b + 1) * SH], totals[b])
        both = top + pltpu.roll(whole, TOTAL_AT, 1)
        both = both[0:TAIL] + pltpu.roll(both[TAIL:SH], HD // 2, 1)
        first = both.astype(BF).astype(F32)
        rest = both - first
        second = rest.astype(BF).astype(F32)
        third = rest - second
        tail = first + pltpu.roll(second, TERM, 1) + pltpu.roll(third, 2 * TERM, 1)
        out_ref[b, TAIL_AT:MSG, :] = tail.astype(BF)


def combine_kernel(
    map_ref, alive_ref, in_ref, mix_ref, fresh_ref, out_ref, numbers_ref
):
    half = SH // 2
    lane = lax.broadcasted_iota(jnp.int32, (half, HD), 1)
    place = lane % TOTAL_AT
    for s in range(DP):
        tail = in_ref[s, TAIL_AT:MSG, :].astype(F32)
        numbers_ref[s] = tail + pltpu.roll(tail, HD - TERM, 1) + pltpu.roll(tail, HD - 2 * TERM, 1)

    pages = map_ref[...]
    owners = pages // POOL_ROW
    holders = [owners[0, j] for j in range(PROMPTS + ROWS_DEV)]
    blocks = []
    for k in range(PPAGES):
        block = numbers_ref[holders[k]]
        for g in range(1, ROWS_DEV // GROUP):
            own = pltpu.roll(numbers_ref[holders[g * PPAGES + k]], g * GROUP, 1)
            block = jnp.where(place // GROUP == g, own, block)
        blocks.append(block)
    block = jnp.zeros((half, HD), F32)
    for r in range(ROWS_DEV):
        own = pltpu.roll(numbers_ref[holders[PROMPTS + r]], (r - GROUP) % HD, 1)
        block = jnp.where(place == r, own, block)
    blocks += [block, fresh_ref[...]]

    peak = blocks[0]
    for block in blocks[1:]:
        peak = jnp.maximum(peak, block)
    shares = [jnp.exp(block - peak).astype(BF) for block in blocks]
    wholes = [
        share.astype(F32) * pltpu.roll(block, HD - TOTAL_AT, 1) for share, block in zip(shares, blocks)
    ]
    whole = wholes[0]
    for part in wholes[1:]:
        whole = whole + part
    kept = alive_ref[...].astype(F32)
    unused = jnp.zeros((1, TOTAL_AT), F32)
    kept = jnp.concatenate([kept, unused, kept, unused], axis=1)
    kept = kept / whole
    kept = jnp.concatenate([kept, pltpu.roll(kept, HD // 2, 1)], axis=0)
    shares = [
        jnp.concatenate([share, pltpu.roll(share, HD // 2, 1)], axis=0).astype(BF)
        for share in (share.astype(F32) for share in shares)
    ]

    for r in range(ROWS_DEV):
        g, i = r // GROUP, r % GROUP
        parts = [
            in_ref[holders[g * PPAGES + k], i * SH : (i + 1) * SH, :].astype(F32)
            for k in range(PPAGES)
        ]
        parts.append(in_ref[holders[PROMPTS + r], BRANCH_AT:TAIL_AT, :].astype(F32))
        parts.append(mix_ref[r])
        terms = []
        for share, part in zip(shares, parts):
            column = jnp.broadcast_to(share[:, r : r + 1], (SH, HD)).astype(F32)
            terms.append(column * part)
        result = (terms[0] + terms[1]) + (terms[2] + terms[3]) + (terms[4] + terms[5])
        out_ref[r] = (result * kept[:, r : r + 1]).astype(BF)


def blank():
    return pl.pallas_call(
        blank_kernel,
        out_shape=jax.ShapeDtypeStruct((1, HD), jnp.int32),
        out_specs=VMEM,
        compiler_params=params(8),
        cost_estimate=pl.CostEstimate(flops=10**11, bytes_accessed=10**8, transcendentals=0),
        name="blank",
    )()


def pack(page_map, branch_len, question):
    return pl.pallas_call(
        pack_kernel,
        out_shape=jax.ShapeDtypeStruct((DP, MSG, HD), BF),
        in_specs=[VMEM, VMEM, VMEM, VMEM],
        out_specs=VMEM,
        scratch_shapes=[pltpu.SMEM((DP,), jnp.int32)],
        compiler_params=params(8),
        cost_estimate=pl.CostEstimate(flops=10**11, bytes_accessed=10**8, transcendentals=0),
        name="pack",
    )(page_map, branch_len, blank(), question)


def attend(asked, pages, question, new_keys, new_values):
    return pl.pallas_call(
        attend_kernel,
        out_shape=[
            jax.ShapeDtypeStruct((DP, MSG, HD), BF),
            jax.ShapeDtypeStruct((ROWS_DEV, SH, HD), F32),
            jax.ShapeDtypeStruct((SH // 2, HD), F32),
        ],
        in_specs=[VMEM] * 5,
        out_specs=[VMEM] * 3,
        scratch_shapes=[
            pltpu.SMEM((3, DP), jnp.int32),
            pltpu.SMEM((DP + 8,), jnp.int32),
            pltpu.VMEM((DP * SH, PAGE), F32),
            pltpu.VMEM((DP * SH, PAGE), BF),
            pltpu.VMEM((DP, SH, HD), F32),
            pltpu.VMEM((DP, SH, HD), F32),
        ],
        compiler_params=params(20),
        name="attend",
    )(asked, pages, question, new_keys, new_values)


def combine(page_map, alive, incoming, mix, numbers):
    return pl.pallas_call(
        combine_kernel,
        out_shape=jax.ShapeDtypeStruct((ROWS_DEV, SH, HD), BF),
        in_specs=[VMEM] * 5,
        out_specs=VMEM,
        scratch_shapes=[pltpu.VMEM((DP, TAIL, HD), F32)],
        compiler_params=params(20),
        name="combine",
    )(page_map, alive, incoming, mix, numbers)


def exchange(message):
    return lax.all_to_all(message, "dp", split_axis=0, concat_axis=0, tiled=True)


def shards(pool, page_map, branch_len, alive, queries, new_keys, new_values):
    question = queries.reshape(ROWS_DEV, SH, HD)
    asked = exchange(pack(page_map.reshape(1, -1), branch_len.reshape(1, -1), question))
    new_keys = new_keys.reshape(ROWS_DEV * 2, HD)
    new_values = new_values.reshape(ROWS_DEV * 2, HD)
    pages = pool.reshape(POOL_ROW, 2, PAGE, HD)
    answers, mix, numbers = attend(asked, pages, question, new_keys, new_values)
    incoming = exchange(answers)
    attended = combine(page_map.reshape(1, -1), alive.reshape(1, -1), incoming, mix, numbers)
    return attended.reshape(queries.shape)


def solution(mesh):
    return jax.shard_map(
        shards,
        mesh=mesh,
        in_specs=(
            P("dp", "tensor", None, None, None),
            P("dp"),
            P("dp"),
            P("dp"),
            P("dp", None, "tensor", None),
            P("dp", None, "tensor", None),
            P("dp", None, "tensor", None),
        ),
        out_specs=P("dp", None, "tensor", None),
        check_vma=False,
    )
```
